256 devices in a mesh: ab: 8 (over y, z_lo), cd: 32 (over z_hi, x, core).
Axes of the slice: x: 4, y: 4, z: 8 (z_hi: 4, z_lo: 2; z = z_hi * 2 + z_lo), core: 2. Of those that a mesh axis runs over, the one named last changes fastest.
Arguments:
- amplitudes: float32 [768, 16384], P('cd', 'ab'), may hold values from -1.25 to 1.25
- driver: float32 [768, 16384], P('cd', 'ab'), may hold values from -6 to 6
- ladder: bfloat16 [16384, 16384], P('ab', 'cd'), may hold values from -0.125 to 0.125
- block_mask: int32 [128, 128], P('ab', 'cd'), may hold values 0 or 1
- pair_list: int32 [768], replicated, may hold values from 0 to 1023, as said below
- occ_energy: float32 [32], replicated, may hold values from -2 to -0.5
- virt_energy: float32 [128], replicated, may hold values from 0.5 to 3
Outputs:
- new_amplitudes: float32 [768, 16384], P('cd', 'ab')
The draws below stay inside these ranges and needn't reach their ends.
Inputs may be any that keep to these rules, and one draw needn't show every extreme that they name: `pair_list`: the entries are distinct occupied pairs i * 32 + j. Rows come in aligned blocks of two: a pair with i != j shares its block with the pair (j, i); pairs with i == j stand two to a block. Pairs 0 and 1023 are always listed.
All inputs are finite; a program needn't handle non-finite values. No bound on the sum of `block_mask` on one device may be relied on, other than what follows from the above.
Results may differ from the reference program's by a relative error of at most 0.008.
Values may be sent and summed in bfloat16 or wider, within the bound.
No kernel may reach another device: no remote copies, remote signals or barrier semaphores. Data moves between devices by JAX's collectives and lax.ppermute only.
A program may use at most 64 MiB of HBM per device.

```python
import jax
import jax.numpy as jnp
import numpy as np
from jax import lax

NV = 128
NOCC = 32
M_PAIRS = 768
BLK = 128
ITERS = 2
NP = 16384
N_AB = 8
N_CD = 32


def draw_pair_list(key, part):
    upper_i, upper_j = np.triu_indices(NOCC, 1)
    diag_even = np.arange(0, NOCC, 2)
    diag_odd = np.arange(1, NOCC, 2)
    lead = np.concatenate([upper_i * NOCC + upper_j, diag_even * NOCC + diag_even]).astype(np.int32)
    trail = np.concatenate([upper_j * NOCC + upper_i, diag_odd * NOCC + diag_odd]).astype(np.int32)
    units = lead.shape[0]
    forced = np.zeros((units,), np.int32)
    forced[units - NOCC // 2] = 1
    forced[units - 1] = 1
    lead_table = jnp.asarray(lead)
    trail_table = jnp.asarray(trail)
    scores = jax.random.randint(jax.random.fold_in(key, 11), (units,), 0, 1 << 16)
    scores = (scores + jnp.asarray(forced) * (1 << 17)) * units + jnp.arange(units, dtype=jnp.int32)
    chosen = lax_top(scores, M_PAIRS // 2)
    shuffle = jax.random.permutation(jax.random.fold_in(key, 12), M_PAIRS // 2)
    chosen = chosen[shuffle]
    turn = jax.random.randint(jax.random.fold_in(key, 13), (M_PAIRS // 2,), 0, 2)
    head = jnp.where(turn == 1, trail_table[chosen], lead_table[chosen])
    tail = jnp.where(turn == 1, lead_table[chosen], trail_table[chosen])
    return jnp.stack([head, tail], axis=1).reshape(M_PAIRS).astype(jnp.int32)


def lax_top(scores, count):
    values, indices = jax.lax.top_k(scores, count)
    return indices.astype(jnp.int32)


def touch_ends(entries, key, smallest, largest):
    extent = entries.shape
    index_at = [jax.random.randint(jax.random.fold_in(key, axis), (), 0, extent[axis]) for axis in range(len(extent))]
    entries = entries.at[tuple(index_at)].set(smallest)
    longest = extent.index(max(extent))
    index_at[longest] = (index_at[longest] + 1) % extent[longest]
    return entries.at[tuple(index_at)].set(largest)


def shard_levels(stream_key, dims, cuts, smallest, high):
    gain = 1.0
    for dim, blocks in cuts:
        heights = jax.random.uniform(jax.random.fold_in(jax.random.fold_in(stream_key, 6), dim), (blocks,), jnp.float32, smallest / len(cuts), high / len(cuts))
        gain = gain * jnp.repeat(jnp.exp(heights), dims[dim] // blocks).reshape((-1,) + (1,) * (len(dims) - 1 - dim))
    return gain


def gaussian(key, extent, deviation, reach, cuts=(), held_as=jnp.bfloat16):
    values = deviation * jax.random.normal(key, extent, jnp.float32)
    if cuts:
        values = values * shard_levels(key, extent, cuts, -0.22, 0.18)
    return jnp.clip(values, -reach, reach).astype(held_as)


def setup_inputs(seed: int = 0) -> dict:
    seeds = jax.random.split(jax.random.key(seed), 8)
    amplitudes = gaussian(seeds[0], (M_PAIRS, NP), 0.2, 1.25, ((0, 32), (1, 8)), jnp.float32)
    driver = gaussian(seeds[1], (M_PAIRS, NP), 1.0, 6.0, ((0, 32), (1, 8)), jnp.float32)
    ladder = gaussian(seeds[2], (NP, NP), (NP // 8) ** -0.5, 0.125, ((0, 8), (1, 32)))
    block_mask = touch_ends((jax.random.randint(seeds[3], (NP // BLK, NP // BLK), 0, 100) < 37).astype(jnp.int32), jax.random.fold_in(seeds[3], 1), 0, 1)
    pair_list = draw_pair_list(jax.random.fold_in(seeds[7], 71), 0)
    occ_energy = jnp.clip(jax.random.uniform(seeds[5], (NOCC,), jnp.float32, -2.0, -0.5), -2.0, -0.5)
    virt_energy = jnp.clip(jax.random.uniform(seeds[6], (NV,), jnp.float32, 0.5, 3.0), 0.5, 3.0)
    return {"amplitudes": amplitudes, "driver": driver, "ladder": ladder, "block_mask": block_mask, "pair_list": pair_list, "occ_energy": occ_energy, "virt_energy": virt_energy}


def pair_maps():
    tile = NV // N_AB
    pairs = jnp.arange(NP, dtype=jnp.int32)
    big_a = pairs // (tile * NV)
    big_b = (pairs // (tile * tile)) % N_AB
    inner_a = (pairs // tile) % tile
    inner_b = pairs % tile
    first = big_a * tile + inner_a
    second = big_b * tile + inner_b
    mirror = big_b * (tile * NV) + big_a * (tile * tile) + inner_b * tile + inner_a
    in_block = NP // N_CD
    piece = NP // (N_AB * N_CD)
    slot = pairs // in_block
    source = (pairs % in_block) // piece
    rest = pairs % piece
    position = source * (NP // N_AB) + slot * piece + rest
    return first, second, mirror, position


def reference(amplitudes, driver, ladder, block_mask, pair_list, occ_energy, virt_energy):
    first, second, mirror, position = pair_maps()
    occ_i = pair_list // NOCC
    occ_j = pair_list % NOCC
    denominator = (virt_energy[first] + virt_energy[second])[None, :] - (occ_energy[occ_i] + occ_energy[occ_j])[:, None]
    inverse = jnp.zeros((NOCC * NOCC,), jnp.int32).at[pair_list].set(jnp.arange(M_PAIRS, dtype=jnp.int32))
    mirror_row = inverse[occ_j * NOCC + occ_i]
    out_block = NP // N_AB
    in_block = NP // N_CD
    ladder_rows = ladder.reshape(N_AB, out_block, NP)
    mask_rows = block_mask.reshape(N_AB, out_block // BLK, NP // BLK)
    state = amplitudes
    for step in range(ITERS):
        low = state.astype(jnp.bfloat16)[:, position].astype(jnp.float32)

        def block_product(operands):
            rows_here, mask_here = operands
            masked = rows_here.astype(jnp.float32).reshape(out_block // BLK, BLK, NP // BLK, BLK)
            masked = masked * mask_here.astype(jnp.float32)[:, None, :, None]
            masked = masked.reshape(out_block, NP)

            def one_block(carry, index):
                start = index * in_block
                left = lax.dynamic_slice_in_dim(low, start, in_block, 1)
                right = lax.dynamic_slice_in_dim(masked, start, in_block, 1)
                part = jnp.dot(left, right.T, precision=lax.Precision.HIGHEST)
                return carry + part.astype(jnp.bfloat16).astype(jnp.float32), None

            zeros = jnp.zeros((M_PAIRS, out_block), jnp.float32)
            total, unused = lax.scan(one_block, zeros, jnp.arange(N_CD, dtype=jnp.int32))
            return total

        blocks = lax.map(block_product, (ladder_rows, mask_rows))
        ladder_term = jnp.transpose(blocks, (1, 0, 2)).reshape(M_PAIRS, NP)
        symmetric = ladder_term + ladder_term[mirror_row][:, mirror]
        state = (driver + symmetric) / denominator
    return state
```

```python
import jax
import jax.numpy as jnp
import numpy as np
from jax import lax
from jax.experimental import pallas as pl
from jax.experimental.pallas import tpu as pltpu
from jax.sharding import Mesh, PartitionSpec as P

NV = 128
NOCC = 32
BLK = 128
BF = jnp.bfloat16
F32 = jnp.float32
AB = ("y", "zl")
GRID = ("x", "zh")
ALL = ("y", "zl", "zh", "x", "core")
VMEM = pl.BlockSpec(memory_space=pltpu.VMEM)
SMEM = pl.BlockSpec(memory_space=pltpu.SMEM)
LIMIT = 48 * 1024 * 1024


def call(kernel, out_shape, inputs, scalars=0, scratch=()):
    specs = [SMEM] * scalars + [VMEM] * (len(inputs) - scalars)
    outs = jax.tree.map(lambda _: VMEM, out_shape)
    return pl.pallas_call(
        kernel,
        out_shape=out_shape,
        in_specs=specs,
        out_specs=outs,
        scratch_shapes=list(scratch),
        compiler_params=pltpu.CompilerParams(vmem_limit_bytes=LIMIT),
    )(*inputs)


def weave_kernel(core_ref, own_ref, other_ref, out_ref):
    first = core_ref[0] == 0
    rows = 256

    def step(i, carry):
        here = pl.ds(pl.multiple_of(i * rows, rows), rows)
        for t in range(own_ref.shape[1] // BLK):
            mine = own_ref[here, t * BLK : (t + 1) * BLK]
            theirs = other_ref[here, t * BLK : (t + 1) * BLK]
            a = jnp.where(first, mine, theirs)
            b = jnp.where(first, theirs, mine)
            half = BLK // 2
            out_ref[here, 2 * t * BLK : (2 * t + 1) * BLK] = jnp.concatenate(
                [a[:, :half], b[:, :half]], axis=1
            )
            out_ref[here, (2 * t + 1) * BLK : (2 * t + 2) * BLK] = jnp.concatenate(
                [a[:, half:], b[:, half:]], axis=1
            )
        return carry

    lax.fori_loop(0, own_ref.shape[0] // rows, step, 0)


def product(low_ref, w_ref, n, width):
    low = jnp.concatenate([low_ref[s] for s in range(low_ref.shape[0])], axis=1)
    w = w_ref[n * width : (n + 1) * width, :]
    return lax.dot_general(low, w, (((1,), (1,)), ((), ())), preferred_element_type=F32)


def columns_kernel(low_ref, w_ref, out_ref):
    n_x = out_ref.shape[0]
    width = 256
    for n in range(w_ref.shape[0] // width):
        part = product(low_ref, w_ref, n, width).astype(BF)
        for j in range(width // BLK):
            q = n * (width // BLK) + j
            out_ref[q % n_x, q // n_x] = part[:, j * BLK : (j + 1) * BLK]


def rows_kernel(low_ref, w_ref, out_ref):
    n_x, rows, _ = out_ref.shape
    width = 256
    for n in range(w_ref.shape[0] // width):
        part = product(low_ref, w_ref, n, width).astype(BF)
        for j in range(n_x):
            out_ref[j, :, n * width : (n + 1) * width] = part[j * rows : (j + 1) * rows]


def sum_leading(ref):
    total = ref[0].astype(F32)
    for i in range(1, ref.shape[0]):
        total = total + ref[i].astype(F32)
    return total


def sum_kernel(pieces_ref, total_ref, low_ref):
    total = sum_leading(pieces_ref)
    total_ref[...] = total
    low_ref[...] = total.astype(BF)


def swap_rows(values, diagonal):
    rows = values.shape[0]
    up = pltpu.roll(values, rows - 1, 0)
    down = pltpu.roll(values, 1, 0)
    even = lax.broadcasted_iota(jnp.int32, values.shape, 0) % 2 == 0
    return jnp.where(diagonal != 0, values, jnp.where(even, up, down))


def close_columns_kernel(half_ref, total_ref, same_ref, cross_ref, drv_ref, den_ref, diag_ref, out_ref):
    half = half_ref[0]
    lane_in = lax.broadcasted_iota(jnp.int32, (BLK, BLK), 0)
    lane_out = lax.broadcasted_iota(jnp.int32, (BLK, BLK), 1)
    goes = lane_in % 16 == half * 8 + lane_out // 16
    yy = lane_out % 16
    same = (goes & (yy == half * 8 + lane_in // 16)).astype(F32).astype(BF)
    cross = (goes & (yy == (1 - half) * 8 + lane_in // 16)).astype(F32).astype(BF)
    mirrored = jnp.dot(same_ref[...], same, preferred_element_type=F32)
    mirrored = mirrored + jnp.dot(cross_ref[...], cross, preferred_element_type=F32)
    mirrored = swap_rows(mirrored, diag_ref[...])
    driver = drv_ref[0].astype(F32) + drv_ref[1].astype(F32)
    low = ((driver + (total_ref[...] + mirrored)) / den_ref[...]).astype(BF)
    for i in range(out_ref.shape[0]):
        out_ref[i] = low


def turn_kernel(pieces_ref, total_ref, out_ref):
    total = sum_leading(pieces_ref)
    total_ref[...] = total
    area = out_ref.shape[2]
    side = 16
    lane_in = lax.broadcasted_iota(jnp.int32, (area, area), 0)
    lane_out = lax.broadcasted_iota(jnp.int32, (area, area), 1)
    turn = (lane_in % side == lane_out // side) & (lane_in // side == lane_out % side)
    turn = turn.astype(F32).astype(BF)
    for b in range(out_ref.shape[0]):
        tile = total[:, b * area : (b + 1) * area].astype(BF)
        out_ref[b] = jnp.dot(tile, turn, preferred_element_type=F32).astype(BF)


def close_rows_kernel(total_ref, tiles_ref, driver_ref, row_ref, col_ref, diag_ref, out_ref):
    area = tiles_ref.shape[2]
    for b in range(tiles_ref.shape[0]):
        here = slice(b * area, (b + 1) * area)
        mirrored = swap_rows(tiles_ref[b].astype(F32), diag_ref[...])
        den = col_ref[:, here] - row_ref[...]
        out_ref[:, here] = (driver_ref[:, here] + (total_ref[:, here] + mirrored)) / den


def pick(table, index):
    hit = index[:, None] == jnp.arange(table.shape[0], dtype=jnp.int32)[None, :]
    return jnp.sum(jnp.where(hit, table[None, :], 0.0), axis=1)


def body(amplitudes, driver, ladder, block_mask, pair_list, occ_energy, virt_energy):
    n_x, n_zh, n_core = lax.axis_size("x"), lax.axis_size("zh"), lax.axis_size("core")
    n_ab = lax.axis_size(AB)
    cells = n_x * n_zh
    core, ix, izh = lax.axis_index("core"), lax.axis_index("x"), lax.axis_index("zh")
    ab_index = lax.axis_index(AB)
    rows, cols = amplitudes.shape
    out_rows, in_cols = ladder.shape
    wide = cols // cells
    many = rows * cells
    side = NV // n_ab
    area = side * side

    def cut(values):
        values = values.reshape(rows, n_zh, n_x, wide)
        return jnp.transpose(values, (2, 1, 0, 3)).reshape(cells, rows, wide)

    masked = ladder.reshape(out_rows // BLK, BLK, in_cols // BLK, BLK)
    masked = (masked * block_mask.astype(BF)[:, None, :, None]).reshape(out_rows, in_cols)
    other = lax.ppermute(masked, "core", [(0, 1), (1, 0)])

    high = lax.reduce_precision(driver, 8, 7)
    pack = jnp.concatenate(
        [cut(amplitudes.astype(BF)), cut(high.astype(BF)), cut((driver - high).astype(BF))], axis=2
    )
    pack = lax.all_to_all(pack, GRID, 0, 0, tiled=True).reshape(many, 3, wide)
    start = pack[:, 0]
    drv = jnp.stack([pack[:, 1], pack[:, 2]])

    weights = call(
        weave_kernel,
        jax.ShapeDtypeStruct((out_rows, 2 * in_cols), BF),
        [core.astype(jnp.int32).reshape(1), masked, other],
        1,
    )

    local = lax.dynamic_index_in_dim(
        pair_list.reshape(n_zh, n_x, n_core, rows), core, 2, keepdims=False
    )
    local = jnp.transpose(local, (1, 0, 2)).reshape(many)
    row_energy = pick(occ_energy, local // NOCC) + pick(occ_energy, local % NOCC)
    diag = (local // NOCC == local % NOCC).astype(jnp.int32)
    pairs = ab_index * cols + jnp.arange(cols, dtype=jnp.int32)
    first = pairs // (side * NV) * side + pairs // side % side
    second = pairs // area % n_ab * side + pairs % side
    col_energy = pick(virt_energy, first) + pick(virt_energy, second)
    cell = izh * n_x + ix
    here = lax.dynamic_slice_in_dim(col_energy, cell * wide, wide)
    den = here[None, :] - row_energy[:, None]
    mine = (ix * n_zh + izh) * rows
    my_rows = lax.dynamic_slice_in_dim(row_energy, mine, rows)
    my_diag = lax.dynamic_slice_in_dim(diag, mine, rows)

    def place(a, q, c):
        return ((a * (n_zh * n_x)) + q) * n_core + c

    same, cross = [], []
    for a in range(n_ab):
        for q in range(cells):
            for c in range(n_core):
                b, h = q // 2, q % 2
                same.append((place(a, q, c), place(b, 2 * a + h, c)))
                cross.append((place(a, q, c), place(b, 2 * a + 1 - h, c)))

    low = lax.all_to_all(jnp.broadcast_to(start[None], (n_ab, many, wide)), AB, 0, 0, tiled=True)
    part = call(columns_kernel, jax.ShapeDtypeStruct((n_x, n_zh, many, wide), BF), [low, weights])
    part = lax.all_to_all(part, "x", 0, 0, tiled=True)
    part = jnp.sum(part.astype(F32), axis=0).astype(BF)
    part = lax.all_to_all(part, "zh", 0, 0, tiled=True)
    total, rounded = call(
        sum_kernel,
        (jax.ShapeDtypeStruct((many, wide), F32), jax.ShapeDtypeStruct((many, wide), BF)),
        [part],
    )
    from_same = lax.ppermute(rounded, ALL, same)
    from_cross = lax.ppermute(rounded, ALL, cross)
    low = call(
        close_columns_kernel,
        jax.ShapeDtypeStruct((n_ab, many, wide), BF),
        [(cell % 2).astype(jnp.int32).reshape(1), total, from_same, from_cross, drv, den, diag[:, None]],
        1,
    )

    low = lax.all_to_all(low, AB, 0, 0, tiled=True)
    part = call(rows_kernel, jax.ShapeDtypeStruct((n_x, many // n_x, cols), BF), [low, weights])
    part = lax.all_to_all(part, "x", 0, 0, tiled=True)
    part = jnp.sum(part.astype(F32), axis=0).astype(BF).reshape(n_zh, rows, cols)
    part = lax.all_to_all(part, "zh", 0, 0, tiled=True)
    total, turned = call(
        turn_kernel,
        (jax.ShapeDtypeStruct((rows, cols), F32), jax.ShapeDtypeStruct((n_ab, rows, area), BF)),
        [part],
    )
    tiles = lax.all_to_all(turned, AB, 0, 0, tiled=True)
    return call(
        close_rows_kernel,
        jax.ShapeDtypeStruct((rows, cols), F32),
        [total, tiles, driver, my_rows[:, None], col_energy[None, :], my_diag[:, None]],
    )


def solution(mesh):
    fine = Mesh(mesh.devices.reshape(4, 2, 4, 4, 2), ALL)
    ab, cd = AB, ("zh", "x", "core")
    placed = (P(cd, ab), P(cd, ab), P(ab, cd), P(ab, cd), P(), P(), P())
    return jax.shard_map(body, mesh=fine, in_specs=placed, out_specs=P(cd, ab), check_vma=False)
```

```python
import jax
import jax.numpy as jnp
from jax import lax
from jax.experimental import pallas as pl
from jax.experimental.pallas import tpu as pltpu
from jax.sharding import Mesh, PartitionSpec as P

NV = 128
NOCC = 32
BLK = 128
SIDE = 16
BF = jnp.bfloat16
F32 = jnp.float32
AB = ("y", "zl")
GRID = ("x", "zh")
ALL = ("y", "zl", "zh", "x", "core")
VMEM = pl.BlockSpec(memory_space=pltpu.VMEM)
ANY = pl.BlockSpec(memory_space=pl.ANY)
SMEM = pl.BlockSpec(memory_space=pltpu.SMEM)
MIB = 1 << 20
SMALL = 12 * MIB
LARGE = 58 * MIB


def shape(*dims, dtype=BF):
    return jax.ShapeDtypeStruct(dims, dtype)


def call(kernel, out_shape, inputs, scalars=0, limit=SMALL):
    specs = [SMEM] * scalars + [VMEM] * (len(inputs) - scalars)
    outs = jax.tree.map(lambda _: VMEM, out_shape)
    return pl.pallas_call(
        kernel,
        out_shape=out_shape,
        in_specs=specs,
        out_specs=outs,
        compiler_params=pltpu.CompilerParams(vmem_limit_bytes=limit),
    )(*inputs)


def ones_where(condition):
    return condition.astype(F32).astype(BF)


def iotas(rows, cols):
    return (
        lax.broadcasted_iota(jnp.int32, (rows, cols), 0),
        lax.broadcasted_iota(jnp.int32, (rows, cols), 1),
    )


def turned(index):
    return index % SIDE * SIDE + index // SIDE


def pack_kernel(amplitudes_hbm, driver_hbm, out_ref, amplitudes_ref, driver_ref, sems):
    n_x, n_zh, _, width = out_ref.shape
    width = width // 2
    step = n_x * width
    copies = []
    for i in range(n_zh):
        here = slice(i * step, (i + 1) * step)
        copies.append(pltpu.make_async_copy(amplitudes_hbm.at[:, here], amplitudes_ref.at[:, here], sems.at[0, i]))
        copies.append(pltpu.make_async_copy(driver_hbm.at[:, here], driver_ref.at[:, here], sems.at[1, i]))
    for copy in copies:
        copy.start()
    for i in range(n_zh):
        copies[2 * i].wait()
        copies[2 * i + 1].wait()
        for x in range(n_x):
            here = slice((i * n_x + x) * width, (i * n_x + x + 1) * width)
            out_ref[x, i, :, :width] = amplitudes_ref[:, here].astype(BF)
            out_ref[x, i, :, width:] = driver_ref[:, here].astype(BF)


def pack_columns(amplitudes, driver, n_x, n_zh):
    rows, cols = amplitudes.shape
    return pl.pallas_call(
        pack_kernel,
        out_shape=shape(n_x, n_zh, rows, 2 * cols // (n_x * n_zh)),
        in_specs=[ANY, ANY],
        out_specs=VMEM,
        scratch_shapes=[pltpu.VMEM((rows, cols), F32)] * 2 + [pltpu.SemaphoreType.DMA((2, n_zh))],
        compiler_params=pltpu.CompilerParams(vmem_limit_bytes=SMALL),
    )(amplitudes, driver)


def mask_kernel(mask_ref, other_mask_ref, ladder_ref, other_ref, out_ref, other_out_ref):
    step = pl.program_id(0) * (ladder_ref.shape[0] // BLK)
    for mask, source, out in ((mask_ref, ladder_ref, out_ref), (other_mask_ref, other_ref, other_out_ref)):
        for i in range(source.shape[0] // BLK):
            rows = slice(i * BLK, (i + 1) * BLK)
            for t in range(source.shape[1] // BLK):
                cols = slice(t * BLK, (t + 1) * BLK)
                block = source[rows, cols]
                out[rows, cols] = jnp.where(mask[t, step + i] != 0, block, jnp.zeros_like(block))


def mask_ladder(block_mask, other_mask, ladder, other):
    rows, cols = ladder.shape
    block = pl.BlockSpec((rows // 4, cols), lambda n: (n, 0))
    return pl.pallas_call(
        mask_kernel,
        grid=(4,),
        out_shape=(shape(rows, cols), shape(rows, cols)),
        in_specs=[SMEM, SMEM, block, block],
        out_specs=(block, block),
        compiler_params=pltpu.CompilerParams(vmem_limit_bytes=LARGE),
        cost_estimate=pl.CostEstimate(flops=1 << 20, bytes_accessed=8 * MIB, transcendentals=0),
    )(block_mask, other_mask, ladder, other)


def send_kernel(mine_ref, masked_ref, turn_ref, *send_refs):
    mine = mine_ref[0]
    area = SIDE * SIDE
    half = area // 2
    count = masked_ref.shape[0] // area
    row, col = iotas(half, area)
    full_row, full_col = iotas(area, area)
    for j in range(count):
        b = lax.rem(mine + j, count)
        tile = masked_ref[pl.ds(pl.multiple_of(b * area, area), area), :]
        if j == 0:
            turn = ones_where(full_col == turned(full_row))
            turn_ref[...] = jnp.dot(turn, tile, preferred_element_type=F32).astype(BF)
        else:
            sent = ones_where(col == jnp.where(mine < b, half + row, turned(row)))
            send_refs[j - 1][...] = jnp.dot(sent, tile, preferred_element_type=F32).astype(BF)


def join_kernel(*refs):
    out_ref = refs[-1]
    at = 0
    for ref in refs[:-1]:
        out_ref[at : at + ref.shape[0], :] = ref[...]
        at += ref.shape[0]


def keep_kernel(mine_ref, own_ref, other_ref, keep_ref):
    mine = mine_ref[0]
    area = SIDE * SIDE
    half = area // 2
    count = own_ref.shape[0] // area
    depth = own_ref.shape[1]
    row, col = iotas(half, area)
    for j in range(count):
        b = lax.rem(mine + j, count)
        kept = ones_where(col == jnp.where(mine < b, row, turned(half + row)))
        for i, ref in enumerate((own_ref, other_ref)):
            cols = slice(i * depth, (i + 1) * depth)
            tile = ref[pl.ds(pl.multiple_of(b * area, area), area), :]
            if j == 0:
                keep_ref[(count - 1) * half :, cols] = tile
            else:
                keep_ref[(j - 1) * half : j * half, cols] = jnp.dot(
                    kept, tile, preferred_element_type=F32
                ).astype(BF)


def times(left, right):
    return lax.dot_general(left, right, (((1,), (1,)), ((), ())), preferred_element_type=F32)


def store_halves(core_ref, low_ref, out_ref):
    first = core_ref[0] == 0
    half = BLK // 2
    count = low_ref.shape[0]
    for s in range(0, count, 2):
        a, b = low_ref[s], low_ref[s + 1]
        zero = jnp.concatenate([a[:, :half], b[:, :half]], axis=1)
        one = jnp.concatenate([a[:, half:], b[:, half:]], axis=1)
        out_ref[:, s // 2 * BLK : (s // 2 + 1) * BLK] = jnp.where(first, zero, one)
        at = (count + s) // 2 * BLK
        out_ref[:, at : at + BLK] = jnp.where(first, one, zero)


def columns_kernel(core_ref, low_ref, own_ref, other_ref, out_ref, held_ref):
    depth = own_ref.shape[1]

    @pl.when(pl.program_id(0) == 0)
    def _():
        store_halves(core_ref, low_ref, held_ref)

    step = 256
    for n in range(own_ref.shape[0] // step):
        here = slice(n * step, (n + 1) * step)
        part = times(held_ref[:, :depth], own_ref[here, :]) + times(held_ref[:, depth:], other_ref[here, :])
        part = part.astype(BF)
        for j in range(step // BLK):
            out_ref[n * (step // BLK) + j, 0] = part[:, j * BLK : (j + 1) * BLK]


def columns_product(which_core, low, own, other, n_x, n_zh):
    n_ab, many, wide = low.shape
    out_rows, depth = own.shape
    block = pl.BlockSpec((out_rows // n_zh, depth), lambda n: (n, 0))
    return pl.pallas_call(
        columns_kernel,
        grid=(n_zh,),
        out_shape=shape(n_x, n_zh, many, wide),
        in_specs=[SMEM, pl.BlockSpec((n_ab, many, wide), lambda n: (0, 0, 0)), block, block],
        out_specs=pl.BlockSpec((n_x, 1, many, wide), lambda n: (0, n, 0, 0)),
        scratch_shapes=[pltpu.VMEM((many, 2 * depth), BF)],
        compiler_params=pltpu.CompilerParams(vmem_limit_bytes=LARGE),
        cost_estimate=pl.CostEstimate(flops=2 << 30, bytes_accessed=7 * MIB, transcendentals=0),
    )(which_core, low, own, other)


def rows_kernel(core_ref, low_ref, diag_ref, keep_ref, mown_ref, mother_ref, out_ref, held_ref, swap_ref):
    n_x, rows, _ = out_ref.shape
    depth = mown_ref.shape[1]

    @pl.when(pl.program_id(0) == 0)
    def _():
        store_halves(core_ref, low_ref, held_ref)
        row, col = iotas(BLK, BLK)
        other = row + 1 - 2 * (row % 2)
        for i in range(held_ref.shape[0] // BLK):
            here = slice(i * BLK, (i + 1) * BLK)
            swap = ones_where(col == jnp.where(diag_ref[here, :] != 0, row, other))
            swap_ref[here, :] = jnp.dot(swap, held_ref[here, :], preferred_element_type=F32).astype(BF)

    part = times(held_ref[...], keep_ref[...])
    part = part + times(swap_ref[:, :depth], mown_ref[...]) + times(swap_ref[:, depth:], mother_ref[...])
    part = part.astype(BF)
    for k in range(n_x):
        out_ref[k] = part[k * rows : (k + 1) * rows]


def rows_product(which_core, low, diag, keep, mown, mother, n_x):
    n_ab, many, wide = low.shape
    width, depth = mown.shape
    step = 384
    block = pl.BlockSpec((step, depth), lambda n: (n, 0))
    return pl.pallas_call(
        rows_kernel,
        grid=(width // step,),
        out_shape=shape(n_x, many // n_x, width),
        in_specs=[
            SMEM,
            pl.BlockSpec((n_ab, many, wide), lambda n: (0, 0, 0)),
            pl.BlockSpec((many, 1), lambda n: (0, 0)),
            pl.BlockSpec((step, 2 * depth), lambda n: (n, 0)),
            block,
            block,
        ],
        out_specs=pl.BlockSpec((n_x, many // n_x, step), lambda n: (0, 0, n)),
        scratch_shapes=[pltpu.VMEM((many, 2 * depth), BF)] * 2,
        compiler_params=pltpu.CompilerParams(vmem_limit_bytes=LARGE),
        cost_estimate=pl.CostEstimate(flops=2 << 30, bytes_accessed=7 * MIB, transcendentals=0),
    )(which_core, low, diag, keep, mown, mother)


def sum_leading(ref):
    total = ref[0].astype(F32)
    for i in range(1, ref.shape[0]):
        total = total + ref[i].astype(F32)
    return total


def swap_rows(values, diagonal):
    rows = values.shape[0]
    up = pltpu.roll(values, rows - 1, 0)
    down = pltpu.roll(values, 1, 0)
    even = lax.broadcasted_iota(jnp.int32, values.shape, 0) % 2 == 0
    return jnp.where(diagonal != 0, values, jnp.where(even, up, down))


def open_columns_kernel(half_ref, pieces_ref, total_ref, same_ref, cross_ref):
    half = half_ref[0]
    total = sum_leading(pieces_ref)
    total_ref[...] = total
    low = total.astype(BF)
    middle = low.shape[0] // 2
    lane, out = iotas(BLK, BLK)
    for ref, which in ((same_ref, half), (cross_ref, 1 - half)):
        y = lane % SIDE
        place = y % 8 * 8 + lane // SIDE
        goes = y // 8 == which
        left = ones_where(goes & (out == place))
        right = ones_where(goes & (out == place + BLK // 2))
        packed = jnp.dot(low[:middle], left, preferred_element_type=F32)
        packed = packed + jnp.dot(low[middle:], right, preferred_element_type=F32)
        ref[...] = packed.astype(BF)


def close_columns_kernel(half_ref, total_ref, same_ref, cross_ref, driver_ref, den_ref, diag_ref, out_ref):
    half = half_ref[0]
    middle = same_ref.shape[0]
    lane, out = iotas(BLK, BLK)
    for part in range(2):
        rows = slice(part * middle, (part + 1) * middle)
        mirrored = 0.0
        for ref, which in ((same_ref, half), (cross_ref, 1 - half)):
            at = lane - part * (BLK // 2)
            inside = (at >= 0) & (at < BLK // 2)
            place = at // 8 * SIDE + which * 8 + at % 8
            spread = ones_where(inside & (out == place))
            mirrored = mirrored + jnp.dot(ref[...], spread, preferred_element_type=F32)
        mirrored = swap_rows(mirrored, diag_ref[rows, :])
        driver = driver_ref[rows, :].astype(F32)
        low = ((driver + (total_ref[rows, :] + mirrored)) / den_ref[rows, :]).astype(BF)
        for i in range(out_ref.shape[0]):
            out_ref[i, rows, :] = low


def open_rows_kernel(mine_ref, pieces_ref, total_ref, out_ref):
    mine = mine_ref[0]
    count, rows, half = out_ref.shape
    total = sum_leading(pieces_ref)
    total_ref[...] = total
    out_ref[mine] = jnp.zeros((rows, half), BF)
    for j in range(1, count):
        out_ref[lax.rem(mine + j, count)] = total[:, (j - 1) * half : j * half].astype(BF)


def close_rows_kernel(mine_ref, total_ref, tiles_ref, driver_ref, row_ref, col_ref, diag_ref, out_ref):
    mine = mine_ref[0]
    count, _, half = tiles_ref.shape
    area = 2 * half
    lane, out = iotas(area, area)
    turn = (lane == turned(out)).astype(F32)
    for j in range(count):
        b = lax.rem(mine + j, count)
        if j == 0:
            symmetric = total_ref[:, (count - 1) * half :]
        else:
            own = total_ref[:, (j - 1) * half : j * half]
            theirs = swap_rows(tiles_ref[b].astype(F32), diag_ref[...])
            behind = jnp.dot(
                jnp.concatenate([theirs, own], axis=1),
                turn,
                precision=lax.Precision.HIGHEST,
                preferred_element_type=F32,
            )
            symmetric = jnp.where(mine < b, jnp.concatenate([own, theirs], axis=1), behind)
        here = pl.ds(pl.multiple_of(b * area, area), area)
        den = col_ref[:, here] - row_ref[...]
        out_ref[:, here] = (driver_ref[:, here] + symmetric) / den


def pick(table, index):
    hit = index[:, None] == jnp.arange(table.shape[0], dtype=jnp.int32)[None, :]
    return jnp.sum(jnp.where(hit, table[None, :], jnp.zeros((), table.dtype)), axis=1)


def body(amplitudes, driver, ladder, block_mask, pair_list, occ_energy, virt_energy):
    n_x, n_zh, n_core = lax.axis_size("x"), lax.axis_size("zh"), lax.axis_size("core")
    n_ab = lax.axis_size(AB)
    cells = n_x * n_zh
    core, ix, izh = lax.axis_index("core"), lax.axis_index("x"), lax.axis_index("zh")
    ab_index = lax.axis_index(AB)
    mine = ab_index.astype(jnp.int32).reshape(1)
    which_core = core.astype(jnp.int32).reshape(1)
    rows, cols = amplitudes.shape
    out_rows, in_cols = ladder.shape
    wide = cols // cells
    many = rows * cells
    area = SIDE * SIDE
    kept = (n_ab - 1) * (area // 2) + area
    swap_core = [(0, 1), (1, 0)]

    pack = pack_columns(amplitudes, driver, n_x, n_zh)
    pack = lax.all_to_all(pack.reshape(cells, rows, 2 * wide), GRID, 0, 0, tiled=True).reshape(many, 2 * wide)
    start = pack[:, :wide]
    drv = pack[:, wide:]

    other = lax.ppermute(ladder, "core", swap_core)
    other_mask = lax.ppermute(block_mask.T, "core", swap_core)
    _, other, other_mask, ladder = lax.optimization_barrier((pack, other, other_mask, ladder))
    own, other = mask_ladder(block_mask.T, other_mask, ladder, other)

    m = jnp.arange(many, dtype=jnp.int32)
    at = m // rows % n_zh * n_x + m // rows // n_zh
    local = pick(pair_list, (at * n_core + core) * rows + m % rows)
    row_energy = pick(occ_energy, local // NOCC) + pick(occ_energy, local % NOCC)
    diag = (local // NOCC == local % NOCC).astype(jnp.int32)
    pairs = ab_index * cols + jnp.arange(cols, dtype=jnp.int32)
    first = pairs // (SIDE * NV) * SIDE + pairs // SIDE % SIDE
    second = pairs // area % n_ab * SIDE + pairs % SIDE
    col_energy = pick(virt_energy, first) + pick(virt_energy, second)
    cell = izh * n_x + ix
    here = lax.dynamic_slice_in_dim(col_energy, cell * wide, wide)
    den = here[None, :] - row_energy[:, None]
    at = (ix * n_zh + izh) * rows
    my_rows = lax.dynamic_slice_in_dim(row_energy, at, rows)
    my_diag = lax.dynamic_slice_in_dim(diag, at, rows)
    half = (cell % 2).astype(jnp.int32).reshape(1)

    def place(a, q, c):
        return ((a * (n_zh * n_x)) + q) * n_core + c

    same, cross = [], []
    for a in range(n_ab):
        for q in range(cells):
            for c in range(n_core):
                b, h = q // 2, q % 2
                same.append((place(a, q, c), place(b, 2 * a + h, c)))
                cross.append((place(a, q, c), place(b, 2 * a + 1 - h, c)))

    low = lax.all_to_all(jnp.broadcast_to(start[None], (n_ab, many, wide)), AB, 0, 0, tiled=True)
    part = columns_product(which_core, low, own, other, n_x, n_zh)
    part, later = lax.optimization_barrier((part, own))
    part = lax.all_to_all(part, "x", 0, 0, tiled=True)

    turn, *send = call(
        send_kernel,
        (shape(area, in_cols),) + (shape(area // 2, in_cols),) * (n_ab - 1),
        [mine, later],
        1,
    )
    slots = [None] * n_ab

    def pass_on(j, block):
        slots[n_ab - j] = lax.ppermute(block, AB, [(k, (k + j) % n_ab) for k in range(n_ab)])

    for j in range(1, n_ab, 2):
        pass_on(j, send[j - 1])
    part, slots[1::2], send = lax.optimization_barrier((part, slots[1::2], send))

    part = jnp.sum(part.astype(F32), axis=0).astype(BF)
    part = lax.all_to_all(part, "zh", 0, 0, tiled=True)
    for j in range(2, n_ab, 2):
        pass_on(j, send[j - 1])
    part, slots[2::2] = lax.optimization_barrier((part, slots[2::2]))
    mirror = call(join_kernel, shape(kept, in_cols), slots[1:] + [turn])
    mirror_other = lax.ppermute(mirror, "core", swap_core)

    total, to_same, to_cross = call(
        open_columns_kernel,
        (shape(many, wide, dtype=F32), shape(many // 2, wide), shape(many // 2, wide)),
        [half, part],
        1,
    )
    from_same = lax.ppermute(to_same, ALL, same)
    from_cross = lax.ppermute(to_cross, ALL, cross)
    low = call(
        close_columns_kernel,
        shape(n_ab, many, wide),
        [half, total, from_same, from_cross, drv, den, diag[:, None]],
        1,
    )

    low, later, later_other = lax.optimization_barrier((low, own, other))
    low = lax.all_to_all(low, AB, 0, 0, tiled=True)
    keep = call(keep_kernel, shape(kept, 2 * in_cols), [mine, later, later_other], 1, LARGE)
    part = rows_product(which_core, low, diag[:, None], keep, mirror, mirror_other, n_x)
    part = lax.all_to_all(part, "x", 0, 0, tiled=True)
    part = jnp.sum(part.astype(F32), axis=0).astype(BF).reshape(n_zh, rows, kept)
    part = lax.all_to_all(part, "zh", 0, 0, tiled=True)
    total, tiles = call(
        open_rows_kernel,
        (shape(rows, kept, dtype=F32), shape(n_ab, rows, area // 2)),
        [mine, part],
        1,
    )
    tiles = lax.all_to_all(tiles, AB, 0, 0, tiled=True)
    return call(
        close_rows_kernel,
        shape(rows, cols, dtype=F32),
        [mine, total, tiles, driver, my_rows[:, None], col_energy[None, :], my_diag[:, None]],
        1,
    )


def solution(mesh):
    fine = Mesh(mesh.devices.reshape(4, 2, 4, 4, 2), ALL)
    ab, cd = AB, ("zh", "x", "core")
    placed = (P(cd, ab), P(cd, ab), P(ab, cd), P(ab, cd), P(), P(), P())
    return jax.shard_map(body, mesh=fine, in_specs=placed, out_specs=P(cd, ab), check_vma=False)
```

```python
import jax
import jax.numpy as jnp
from jax import lax
from jax.experimental import pallas as pl
from jax.experimental.pallas import tpu as pltpu
from jax.sharding import Mesh, PartitionSpec as P

NV = 128
NOCC = 32
BLK = 128
SIDE = 16
BF = jnp.bfloat16
F32 = jnp.float32
AB = ("y", "zl")
GRID = ("x", "zh")
ALL = ("y", "zl", "zh", "x", "core")
VMEM = pl.BlockSpec(memory_space=pltpu.VMEM)
ANY = pl.BlockSpec(memory_space=pl.ANY)
SMEM = pl.BlockSpec(memory_space=pltpu.SMEM)
MIB = 1 << 20
SMALL = 12 * MIB
LARGE = 52 * MIB
WHOLE = 60 * MIB


def shape(*dims, dtype=BF):
    return jax.ShapeDtypeStruct(dims, dtype)


def call(kernel, out_shape, inputs, scalars=0, limit=SMALL):
    specs = [SMEM] * scalars + [VMEM] * (len(inputs) - scalars)
    outs = jax.tree.map(lambda _: VMEM, out_shape)
    return pl.pallas_call(
        kernel,
        out_shape=out_shape,
        in_specs=specs,
        out_specs=outs,
        compiler_params=pltpu.CompilerParams(vmem_limit_bytes=limit),
    )(*inputs)


def ones_where(condition):
    return condition.astype(F32).astype(BF)


def iotas(rows, cols):
    return (
        lax.broadcasted_iota(jnp.int32, (rows, cols), 0),
        lax.broadcasted_iota(jnp.int32, (rows, cols), 1),
    )


def turned(index):
    return index % SIDE * SIDE + index // SIDE


def pack_kernel(amplitudes_hbm, driver_hbm, out_ref, amplitudes_ref, driver_ref, sems):
    n_x, n_zh, _, width = out_ref.shape
    width = width // 2
    step = n_x * width
    copies = []
    for i in range(n_zh):
        here = slice(i * step, (i + 1) * step)
        copies.append(pltpu.make_async_copy(amplitudes_hbm.at[:, here], amplitudes_ref.at[:, here], sems.at[0, i]))
        copies.append(pltpu.make_async_copy(driver_hbm.at[:, here], driver_ref.at[:, here], sems.at[1, i]))
    for copy in copies:
        copy.start()
    for i in range(n_zh):
        copies[2 * i].wait()
        copies[2 * i + 1].wait()
        for x in range(n_x):
            here = slice((i * n_x + x) * width, (i * n_x + x + 1) * width)
            out_ref[x, i, :, :width] = amplitudes_ref[:, here].astype(BF)
            out_ref[x, i, :, width:] = driver_ref[:, here].astype(BF)


def pack_columns(amplitudes, driver, n_x, n_zh):
    rows, cols = amplitudes.shape
    return pl.pallas_call(
        pack_kernel,
        out_shape=shape(n_x, n_zh, rows, 2 * cols // (n_x * n_zh)),
        in_specs=[ANY, ANY],
        out_specs=VMEM,
        scratch_shapes=[pltpu.VMEM((rows, cols), F32)] * 2 + [pltpu.SemaphoreType.DMA((2, n_zh))],
        compiler_params=pltpu.CompilerParams(vmem_limit_bytes=WHOLE),
    )(amplitudes, driver)


def mask_kernel(mask_ref, other_mask_ref, ladder_ref, other_ref, out_ref, other_out_ref):
    step = pl.program_id(0) * (ladder_ref.shape[0] // BLK)
    for mask, source, out in ((mask_ref, ladder_ref, out_ref), (other_mask_ref, other_ref, other_out_ref)):
        for i in range(source.shape[0] // BLK):
            rows = slice(i * BLK, (i + 1) * BLK)
            for t in range(source.shape[1] // BLK):
                cols = slice(t * BLK, (t + 1) * BLK)
                block = source[rows, cols]
                out[rows, cols] = jnp.where(mask[t, step + i] != 0, block, jnp.zeros_like(block))


def mask_ladder(block_mask, other_mask, ladder, other):
    rows, cols = ladder.shape
    block = pl.BlockSpec((rows // 4, cols), lambda n: (n, 0))
    return pl.pallas_call(
        mask_kernel,
        grid=(4,),
        out_shape=(shape(rows, cols), shape(rows, cols)),
        in_specs=[SMEM, SMEM, block, block],
        out_specs=(block, block),
        compiler_params=pltpu.CompilerParams(vmem_limit_bytes=LARGE),
        cost_estimate=pl.CostEstimate(flops=1 << 20, bytes_accessed=8 * MIB, transcendentals=0),
    )(block_mask, other_mask, ladder, other)


def send_kernel(mine_ref, masked_ref, turn_ref, *send_refs):
    mine = mine_ref[0]
    area = SIDE * SIDE
    half = area // 2
    count = masked_ref.shape[0] // area
    row, col = iotas(half, area)
    full_row, full_col = iotas(area, area)
    for j in range(count):
        b = lax.rem(mine + j, count)
        tile = masked_ref[pl.ds(pl.multiple_of(b * area, area), area), :]
        if j == 0:
            turn = ones_where(full_col == turned(full_row))
            turn_ref[...] = jnp.dot(turn, tile, preferred_element_type=F32).astype(BF)
        else:
            sent = ones_where(col == jnp.where(mine < b, half + row, turned(row)))
            send_refs[j - 1][...] = jnp.dot(sent, tile, preferred_element_type=F32).astype(BF)


def join_kernel(*refs):
    out_ref = refs[-1]
    at = 0
    for ref in refs[:-1]:
        out_ref[at : at + ref.shape[0], :] = ref[...]
        at += ref.shape[0]


def keep_kernel(mine_ref, own_ref, other_ref, keep_ref):
    mine = mine_ref[0]
    area = SIDE * SIDE
    half = area // 2
    count = own_ref.shape[0] // area
    depth = own_ref.shape[1]
    row, col = iotas(half, area)
    for j in range(count):
        b = lax.rem(mine + j, count)
        kept = ones_where(col == jnp.where(mine < b, row, turned(half + row)))
        for i, ref in enumerate((own_ref, other_ref)):
            cols = slice(i * depth, (i + 1) * depth)
            tile = ref[pl.ds(pl.multiple_of(b * area, area), area), :]
            if j == 0:
                keep_ref[(count - 1) * half :, cols] = tile
            else:
                keep_ref[(j - 1) * half : j * half, cols] = jnp.dot(
                    kept, tile, preferred_element_type=F32
                ).astype(BF)


def times(left, right):
    return lax.dot_general(left, right, (((1,), (1,)), ((), ())), preferred_element_type=F32)


def store_halves(core_ref, low_ref, out_ref):
    first = core_ref[0] == 0
    half = BLK // 2
    count = low_ref.shape[0]
    for s in range(0, count, 2):
        a, b = low_ref[s], low_ref[s + 1]
        zero = jnp.concatenate([a[:, :half], b[:, :half]], axis=1)
        one = jnp.concatenate([a[:, half:], b[:, half:]], axis=1)
        out_ref[:, s // 2 * BLK : (s // 2 + 1) * BLK] = jnp.where(first, zero, one)
        at = (count + s) // 2 * BLK
        out_ref[:, at : at + BLK] = jnp.where(first, one, zero)


def columns_kernel(core_ref, low_ref, own_ref, other_ref, out_ref, held_ref):
    depth = own_ref.shape[1]

    @pl.when(pl.program_id(0) == 0)
    def _():
        store_halves(core_ref, low_ref, held_ref)

    count = out_ref.shape[0] * out_ref.shape[1]
    part = times(held_ref[:, :depth], own_ref[...]) + times(held_ref[:, depth:], other_ref[...])
    part = part.astype(BF)
    for j in range(count):
        out_ref[j % out_ref.shape[0], j // out_ref.shape[0]] = part[:, j * BLK : (j + 1) * BLK]


def columns_product(which_core, low, own, other, n_x, n_zh):
    n_ab, many, wide = low.shape
    out_rows, depth = own.shape
    steps = 2
    block = pl.BlockSpec((out_rows // steps, depth), lambda n: (n, 0))
    return pl.pallas_call(
        columns_kernel,
        grid=(steps,),
        out_shape=shape(n_x, n_zh, many, wide),
        in_specs=[SMEM, pl.BlockSpec((n_ab, many, wide), lambda n: (0, 0, 0)), block, block],
        out_specs=pl.BlockSpec((n_x, n_zh // steps, many, wide), lambda n: (0, n, 0, 0)),
        scratch_shapes=[pltpu.VMEM((many, 2 * depth), BF)],
        compiler_params=pltpu.CompilerParams(vmem_limit_bytes=LARGE),
        cost_estimate=pl.CostEstimate(flops=2 << 30, bytes_accessed=7 * MIB, transcendentals=0),
    )(which_core, low, own, other)


def rows_kernel(core_ref, low_ref, diag_ref, keep_ref, mown_ref, mother_ref, out_ref, held_ref, swap_ref):
    n_x, rows, _ = out_ref.shape
    depth = mown_ref.shape[1]

    @pl.when(pl.program_id(0) == 0)
    def _():
        store_halves(core_ref, low_ref, held_ref)
        row, col = iotas(BLK, BLK)
        other = row + 1 - 2 * (row % 2)
        for i in range(held_ref.shape[0] // BLK):
            here = slice(i * BLK, (i + 1) * BLK)
            swap = ones_where(col == jnp.where(diag_ref[here, :] != 0, row, other))
            swap_ref[here, :] = jnp.dot(swap, held_ref[here, :], preferred_element_type=F32).astype(BF)

    part = times(held_ref[...], keep_ref[...])
    part = part + times(swap_ref[:, :depth], mown_ref[...]) + times(swap_ref[:, depth:], mother_ref[...])
    part = part.astype(BF)
    for k in range(n_x):
        out_ref[k] = part[k * rows : (k + 1) * rows]


def rows_product(which_core, low, diag, keep, mown, mother, n_x):
    n_ab, many, wide = low.shape
    width, depth = mown.shape
    step = 384
    block = pl.BlockSpec((step, depth), lambda n: (n, 0))
    return pl.pallas_call(
        rows_kernel,
        grid=(width // step,),
        out_shape=shape(n_x, many // n_x, width),
        in_specs=[
            SMEM,
            pl.BlockSpec((n_ab, many, wide), lambda n: (0, 0, 0)),
            pl.BlockSpec((many, 1), lambda n: (0, 0)),
            pl.BlockSpec((step, 2 * depth), lambda n: (n, 0)),
            block,
            block,
        ],
        out_specs=pl.BlockSpec((n_x, many // n_x, step), lambda n: (0, 0, n)),
        scratch_shapes=[pltpu.VMEM((many, 2 * depth), BF)] * 2,
        compiler_params=pltpu.CompilerParams(vmem_limit_bytes=LARGE),
        cost_estimate=pl.CostEstimate(flops=2 << 30, bytes_accessed=7 * MIB, transcendentals=0),
    )(which_core, low, diag, keep, mown, mother)


def sum_leading(ref):
    total = ref[0].astype(F32)
    for i in range(1, ref.shape[0]):
        total = total + ref[i].astype(F32)
    return total


def gather_sum_kernel(parts_hbm, out_ref, parts_ref, sems):
    copies = []
    for j in range(out_ref.shape[0]):
        copies.append(pltpu.make_async_copy(parts_hbm.at[:, j], parts_ref.at[:, j], sems.at[j]))
        copies[-1].start()
    for j in range(out_ref.shape[0]):
        copies[j].wait()
        total = parts_ref[0, j].astype(F32)
        for i in range(1, parts_ref.shape[0]):
            total = total + parts_ref[i, j].astype(F32)
        out_ref[j] = total.astype(BF)


def sum_sources(parts):
    return pl.pallas_call(
        gather_sum_kernel,
        out_shape=shape(*parts.shape[1:]),
        in_specs=[ANY],
        out_specs=VMEM,
        scratch_shapes=[pltpu.VMEM(parts.shape, BF), pltpu.SemaphoreType.DMA((parts.shape[1],))],
        compiler_params=pltpu.CompilerParams(vmem_limit_bytes=WHOLE),
    )(parts)


def swap_rows(values, diagonal):
    rows = values.shape[0]
    up = pltpu.roll(values, rows - 1, 0)
    down = pltpu.roll(values, 1, 0)
    even = lax.broadcasted_iota(jnp.int32, values.shape, 0) % 2 == 0
    return jnp.where(diagonal != 0, values, jnp.where(even, up, down))


def open_columns_kernel(half_ref, pieces_ref, total_ref, same_ref, cross_ref):
    half = half_ref[0]
    total = sum_leading(pieces_ref)
    total_ref[...] = total
    low = total.astype(BF)
    middle = low.shape[0] // 2
    lane, out = iotas(BLK, BLK)
    for ref, which in ((same_ref, half), (cross_ref, 1 - half)):
        y = lane % SIDE
        place = y % 8 * 8 + lane // SIDE
        goes = y // 8 == which
        left = ones_where(goes & (out == place))
        right = ones_where(goes & (out == place + BLK // 2))
        packed = jnp.dot(low[:middle], left, preferred_element_type=F32)
        packed = packed + jnp.dot(low[middle:], right, preferred_element_type=F32)
        ref[...] = packed.astype(BF)


def close_columns_kernel(half_ref, total_ref, same_ref, cross_ref, driver_ref, den_ref, diag_ref, out_ref):
    half = half_ref[0]
    middle = same_ref.shape[0]
    lane, out = iotas(BLK, BLK)
    for part in range(2):
        rows = slice(part * middle, (part + 1) * middle)
        mirrored = 0.0
        for ref, which in ((same_ref, half), (cross_ref, 1 - half)):
            at = lane - part * (BLK // 2)
            inside = (at >= 0) & (at < BLK // 2)
            place = at // 8 * SIDE + which * 8 + at % 8
            spread = ones_where(inside & (out == place))
            mirrored = mirrored + jnp.dot(ref[...], spread, preferred_element_type=F32)
        mirrored = swap_rows(mirrored, diag_ref[rows, :])
        driver = driver_ref[rows, :].astype(F32)
        low = ((driver + (total_ref[rows, :] + mirrored)) / den_ref[rows, :]).astype(BF)
        for i in range(out_ref.shape[0]):
            out_ref[i, rows, :] = low


def open_rows_kernel(mine_ref, pieces_ref, total_ref, out_ref):
    mine = mine_ref[0]
    count, rows, half = out_ref.shape
    total = sum_leading(pieces_ref)
    total_ref[...] = total
    out_ref[mine] = jnp.zeros((rows, half), BF)
    for j in range(1, count):
        out_ref[lax.rem(mine + j, count)] = total[:, (j - 1) * half : j * half].astype(BF)


def close_rows_kernel(mine_ref, total_ref, tiles_ref, driver_ref, row_ref, col_ref, diag_ref, out_ref):
    mine = mine_ref[0]
    count, _, half = tiles_ref.shape
    area = 2 * half
    lane, out = iotas(area, area)
    turn = (lane == turned(out)).astype(F32)
    for j in range(count):
        b = lax.rem(mine + j, count)
        if j == 0:
            symmetric = total_ref[:, (count - 1) * half :]
        else:
            own = total_ref[:, (j - 1) * half : j * half]
            theirs = swap_rows(tiles_ref[b].astype(F32), diag_ref[...])
            behind = jnp.dot(
                jnp.concatenate([theirs, own], axis=1),
                turn,
                precision=lax.Precision.HIGHEST,
                preferred_element_type=F32,
            )
            symmetric = jnp.where(mine < b, jnp.concatenate([own, theirs], axis=1), behind)
        here = pl.ds(pl.multiple_of(b * area, area), area)
        den = col_ref[:, here] - row_ref[...]
        out_ref[:, here] = (driver_ref[:, here] + symmetric) / den


def pick(table, index):
    hit = index[:, None] == jnp.arange(table.shape[0], dtype=jnp.int32)[None, :]
    return jnp.sum(jnp.where(hit, table[None, :], jnp.zeros((), table.dtype)), axis=1)


def body(amplitudes, driver, ladder, block_mask, pair_list, occ_energy, virt_energy):
    n_x, n_zh, n_core = lax.axis_size("x"), lax.axis_size("zh"), lax.axis_size("core")
    n_ab = lax.axis_size(AB)
    cells = n_x * n_zh
    core, ix, izh = lax.axis_index("core"), lax.axis_index("x"), lax.axis_index("zh")
    ab_index = lax.axis_index(AB)
    mine = ab_index.astype(jnp.int32).reshape(1)
    which_core = core.astype(jnp.int32).reshape(1)
    rows, cols = amplitudes.shape
    out_rows, in_cols = ladder.shape
    wide = cols // cells
    many = rows * cells
    area = SIDE * SIDE
    kept = (n_ab - 1) * (area // 2) + area
    swap_core = [(0, 1), (1, 0)]

    pack = pack_columns(amplitudes, driver, n_x, n_zh)
    pack = lax.all_to_all(pack.reshape(cells, rows, 2 * wide), GRID, 0, 0, tiled=True).reshape(many, 2 * wide)
    start = pack[:, :wide]
    drv = pack[:, wide:]

    other = lax.ppermute(ladder, "core", swap_core)
    other_mask = lax.ppermute(block_mask.T, "core", swap_core)
    _, other, other_mask, ladder = lax.optimization_barrier((pack, other, other_mask, ladder))
    own, other = mask_ladder(block_mask.T, other_mask, ladder, other)

    m = jnp.arange(many, dtype=jnp.int32)
    at = m // rows % n_zh * n_x + m // rows // n_zh
    local = pick(pair_list, (at * n_core + core) * rows + m % rows)
    row_energy = pick(occ_energy, local // NOCC) + pick(occ_energy, local % NOCC)
    diag = (local // NOCC == local % NOCC).astype(jnp.int32)
    pairs = ab_index * cols + jnp.arange(cols, dtype=jnp.int32)
    first = pairs // (SIDE * NV) * SIDE + pairs // SIDE % SIDE
    second = pairs // area % n_ab * SIDE + pairs % SIDE
    col_energy = pick(virt_energy, first) + pick(virt_energy, second)
    cell = izh * n_x + ix
    here = lax.dynamic_slice_in_dim(col_energy, cell * wide, wide)
    den = here[None, :] - row_energy[:, None]
    at = (ix * n_zh + izh) * rows
    my_rows = lax.dynamic_slice_in_dim(row_energy, at, rows)
    my_diag = lax.dynamic_slice_in_dim(diag, at, rows)
    half = (cell % 2).astype(jnp.int32).reshape(1)

    def place(a, q, c):
        return ((a * (n_zh * n_x)) + q) * n_core + c

    same, cross = [], []
    for a in range(n_ab):
        for q in range(cells):
            for c in range(n_core):
                b, h = q // 2, q % 2
                same.append((place(a, q, c), place(b, 2 * a + h, c)))
                cross.append((place(a, q, c), place(b, 2 * a + 1 - h, c)))

    low = lax.all_to_all(jnp.broadcast_to(start[None], (n_ab, many, wide)), AB, 0, 0, tiled=True)
    part = columns_product(which_core, low, own, other, n_x, n_zh)
    part, later = lax.optimization_barrier((part, own))
    part = lax.all_to_all(part, "x", 0, 0, tiled=True)

    turn, *send = call(
        send_kernel,
        (shape(area, in_cols),) + (shape(area // 2, in_cols),) * (n_ab - 1),
        [mine, later],
        1,
    )
    slots = [None] * n_ab

    def pass_on(j, block):
        slots[n_ab - j] = lax.ppermute(block, AB, [(k, (k + j) % n_ab) for k in range(n_ab)])

    for j in range(1, n_ab, 2):
        pass_on(j, send[j - 1])
    part, slots[1::2], send = lax.optimization_barrier((part, slots[1::2], send))

    part = lax.all_to_all(sum_sources(part), "zh", 0, 0, tiled=True)
    for j in range(2, n_ab, 2):
        pass_on(j, send[j - 1])
    part, slots[2::2] = lax.optimization_barrier((part, slots[2::2]))
    mirror = call(join_kernel, shape(kept, in_cols), slots[1:] + [turn])
    mirror_other = lax.ppermute(mirror, "core", swap_core)

    total, to_same, to_cross = call(
        open_columns_kernel,
        (shape(many, wide, dtype=F32), shape(many // 2, wide), shape(many // 2, wide)),
        [half, part],
        1,
    )
    from_same = lax.ppermute(to_same, ALL, same)
    from_cross = lax.ppermute(to_cross, ALL, cross)
    low = call(
        close_columns_kernel,
        shape(n_ab, many, wide),
        [half, total, from_same, from_cross, drv, den, diag[:, None]],
        1,
    )

    low, later, later_other = lax.optimization_barrier((low, own, other))
    low = lax.all_to_all(low, AB, 0, 0, tiled=True)
    keep = call(keep_kernel, shape(kept, 2 * in_cols), [mine, later, later_other], 1, LARGE)
    part = rows_product(which_core, low, diag[:, None], keep, mirror, mirror_other, n_x)
    part = lax.all_to_all(part, "x", 0, 0, tiled=True)
    part = jnp.sum(part.astype(F32), axis=0).astype(BF).reshape(n_zh, rows, kept)
    part = lax.all_to_all(part, "zh", 0, 0, tiled=True)
    total, tiles = call(
        open_rows_kernel,
        (shape(rows, kept, dtype=F32), shape(n_ab, rows, area // 2)),
        [mine, part],
        1,
    )
    tiles = lax.all_to_all(tiles, AB, 0, 0, tiled=True)
    return call(
        close_rows_kernel,
        shape(rows, cols, dtype=F32),
        [mine, total, tiles, driver, my_rows[:, None], col_energy[None, :], my_diag[:, None]],
        1,
    )


def solution(mesh):
    fine = Mesh(mesh.devices.reshape(4, 2, 4, 4, 2), ALL)
    ab, cd = AB, ("zh", "x", "core")
    placed = (P(cd, ab), P(cd, ab), P(ab, cd), P(ab, cd), P(), P(), P())
    return jax.shard_map(body, mesh=fine, in_specs=placed, out_specs=P(cd, ab), check_vma=False)
```

```python
import jax
import jax.numpy as jnp
from jax import lax
from jax.experimental import pallas as pl
from jax.experimental.pallas import tpu as pltpu
from jax.sharding import Mesh, PartitionSpec as P

NV = 128
NOCC = 32
BLK = 128
SIDE = 16
BF = jnp.bfloat16
F32 = jnp.float32
AB = ("y", "zl")
GRID = ("x", "zh")
ALL = ("y", "zl", "zh", "x", "core")
VMEM = pl.BlockSpec(memory_space=pltpu.VMEM)
ANY = pl.BlockSpec(memory_space=pl.ANY)
SMEM = pl.BlockSpec(memory_space=pltpu.SMEM)
MIB = 1 << 20
SMALL = 12 * MIB
LARGE = 52 * MIB
WHOLE = 60 * MIB


def shape(*dims, dtype=BF):
    return jax.ShapeDtypeStruct(dims, dtype)


def call(kernel, out_shape, inputs, scalars=0, limit=SMALL):
    specs = [SMEM] * scalars + [VMEM] * (len(inputs) - scalars)
    outs = jax.tree.map(lambda _: VMEM, out_shape)
    return pl.pallas_call(
        kernel,
        out_shape=out_shape,
        in_specs=specs,
        out_specs=outs,
        compiler_params=pltpu.CompilerParams(vmem_limit_bytes=limit),
    )(*inputs)


def ones_where(condition):
    return condition.astype(F32).astype(BF)


def iotas(rows, cols):
    return (
        lax.broadcasted_iota(jnp.int32, (rows, cols), 0),
        lax.broadcasted_iota(jnp.int32, (rows, cols), 1),
    )


def turned(index):
    return index % SIDE * SIDE + index // SIDE


def pack_kernel(amplitudes_hbm, driver_hbm, out_ref, amplitudes_ref, driver_ref, sems):
    n_x, n_zh, _, width = out_ref.shape
    width = width // 2
    step = n_x * width
    copies = []
    for i in range(n_zh):
        here = slice(i * step, (i + 1) * step)
        copies.append(pltpu.make_async_copy(amplitudes_hbm.at[:, here], amplitudes_ref.at[:, here], sems.at[0, i]))
        copies.append(pltpu.make_async_copy(driver_hbm.at[:, here], driver_ref.at[:, here], sems.at[1, i]))
    for copy in copies:
        copy.start()
    for i in range(n_zh):
        copies[2 * i].wait()
        copies[2 * i + 1].wait()
        for x in range(n_x):
            here = slice((i * n_x + x) * width, (i * n_x + x + 1) * width)
            out_ref[x, i, :, :width] = amplitudes_ref[:, here].astype(BF)
            out_ref[x, i, :, width:] = driver_ref[:, here].astype(BF)


def pack_columns(amplitudes, driver, n_x, n_zh):
    rows, cols = amplitudes.shape
    return pl.pallas_call(
        pack_kernel,
        out_shape=shape(n_x, n_zh, rows, 2 * cols // (n_x * n_zh)),
        in_specs=[ANY, ANY],
        out_specs=VMEM,
        scratch_shapes=[pltpu.VMEM((rows, cols), F32)] * 2 + [pltpu.SemaphoreType.DMA((2, n_zh))],
        compiler_params=pltpu.CompilerParams(vmem_limit_bytes=WHOLE),
    )(amplitudes, driver)


def mask_kernel(mask_ref, other_mask_ref, ladder_ref, other_ref, out_ref, other_out_ref):
    step = pl.program_id(0) * (ladder_ref.shape[0] // BLK)
    for mask, source, out in ((mask_ref, ladder_ref, out_ref), (other_mask_ref, other_ref, other_out_ref)):
        for i in range(source.shape[0] // BLK):
            rows = slice(i * BLK, (i + 1) * BLK)
            for t in range(source.shape[1] // BLK):
                cols = slice(t * BLK, (t + 1) * BLK)
                block = source[rows, cols]
                out[rows, cols] = jnp.where(mask[t, step + i] != 0, block, jnp.zeros_like(block))


def mask_ladder(block_mask, other_mask, ladder, other):
    rows, cols = ladder.shape
    block = pl.BlockSpec((rows // 4, cols), lambda n: (n, 0))
    return pl.pallas_call(
        mask_kernel,
        grid=(4,),
        out_shape=(shape(rows, cols), shape(rows, cols)),
        in_specs=[SMEM, SMEM, block, block],
        out_specs=(block, block),
        compiler_params=pltpu.CompilerParams(vmem_limit_bytes=LARGE),
        cost_estimate=pl.CostEstimate(flops=1 << 20, bytes_accessed=8 * MIB, transcendentals=0),
    )(block_mask, other_mask, ladder, other)


def send_kernel(mine_ref, masked_ref, turn_ref, *send_refs):
    mine = mine_ref[0]
    area = SIDE * SIDE
    half = area // 2
    count = masked_ref.shape[0] // area
    row, col = iotas(half, area)
    full_row, full_col = iotas(area, area)
    for j in range(count):
        b = lax.rem(mine + j, count)
        tile = masked_ref[pl.ds(pl.multiple_of(b * area, area), area), :]
        if j == 0:
            turn = ones_where(full_col == turned(full_row))
            turn_ref[...] = jnp.dot(turn, tile, preferred_element_type=F32).astype(BF)
        else:
            sent = ones_where(col == jnp.where(mine < b, half + row, turned(row)))
            send_refs[j - 1][...] = jnp.dot(sent, tile, preferred_element_type=F32).astype(BF)


def join_kernel(*refs):
    out_ref = refs[-1]
    at = 0
    for ref in refs[:-1]:
        out_ref[at : at + ref.shape[0], :] = ref[...]
        at += ref.shape[0]


def keep_kernel(mine_ref, own_ref, other_ref, keep_ref):
    mine = mine_ref[0]
    area = SIDE * SIDE
    half = area // 2
    count = own_ref.shape[0] // area
    depth = own_ref.shape[1]
    row, col = iotas(half, area)
    for j in range(count):
        b = lax.rem(mine + j, count)
        kept = ones_where(col == jnp.where(mine < b, row, turned(half + row)))
        for i, ref in enumerate((own_ref, other_ref)):
            cols = slice(i * depth, (i + 1) * depth)
            tile = ref[pl.ds(pl.multiple_of(b * area, area), area), :]
            if j == 0:
                keep_ref[(count - 1) * half :, cols] = tile
            else:
                keep_ref[(j - 1) * half : j * half, cols] = jnp.dot(
                    kept, tile, preferred_element_type=F32
                ).astype(BF)


def times(left, right):
    return lax.dot_general(left, right, (((1,), (1,)), ((), ())), preferred_element_type=F32)


def store_halves(core_ref, low_ref, out_ref):
    first = core_ref[0] == 0
    half = BLK // 2
    count = low_ref.shape[0]
    for s in range(0, count, 2):
        a, b = low_ref[s], low_ref[s + 1]
        zero = jnp.concatenate([a[:, :half], b[:, :half]], axis=1)
        one = jnp.concatenate([a[:, half:], b[:, half:]], axis=1)
        out_ref[:, s // 2 * BLK : (s // 2 + 1) * BLK] = jnp.where(first, zero, one)
        at = (count + s) // 2 * BLK
        out_ref[:, at : at + BLK] = jnp.where(first, one, zero)


def columns_kernel(core_ref, low_ref, own_ref, other_ref, out_ref, held_ref):
    depth = own_ref.shape[1]

    @pl.when(pl.program_id(0) == 0)
    def _():
        store_halves(core_ref, low_ref, held_ref)

    count = out_ref.shape[0] * out_ref.shape[1]
    part = times(held_ref[:, :depth], own_ref[...]) + times(held_ref[:, depth:], other_ref[...])
    part = part.astype(BF)
    for j in range(count):
        out_ref[j % out_ref.shape[0], j // out_ref.shape[0]] = part[:, j * BLK : (j + 1) * BLK]


def columns_product(which_core, low, own, other, n_x, n_zh):
    n_ab, many, wide = low.shape
    out_rows, depth = own.shape
    steps = 2
    block = pl.BlockSpec((out_rows // steps, depth), lambda n: (n, 0))
    return pl.pallas_call(
        columns_kernel,
        grid=(steps,),
        out_shape=shape(n_x, n_zh, many, wide),
        in_specs=[SMEM, pl.BlockSpec((n_ab, many, wide), lambda n: (0, 0, 0)), block, block],
        out_specs=pl.BlockSpec((n_x, n_zh // steps, many, wide), lambda n: (0, n, 0, 0)),
        scratch_shapes=[pltpu.VMEM((many, 2 * depth), BF)],
        compiler_params=pltpu.CompilerParams(vmem_limit_bytes=LARGE),
        cost_estimate=pl.CostEstimate(flops=2 << 30, bytes_accessed=7 * MIB, transcendentals=0),
    )(which_core, low, own, other)


def rows_kernel(core_ref, low_ref, diag_ref, keep_ref, mown_ref, mother_ref, out_ref, held_ref, swap_ref):
    n_x, rows, _ = out_ref.shape
    depth = mown_ref.shape[1]

    @pl.when(pl.program_id(0) == 0)
    def _():
        store_halves(core_ref, low_ref, held_ref)
        row, col = iotas(BLK, BLK)
        other = row + 1 - 2 * (row % 2)
        for i in range(held_ref.shape[0] // BLK):
            here = slice(i * BLK, (i + 1) * BLK)
            swap = ones_where(col == jnp.where(diag_ref[here, :] != 0, row, other))
            swap_ref[here, :] = jnp.dot(swap, held_ref[here, :], preferred_element_type=F32).astype(BF)

    part = times(held_ref[...], keep_ref[...])
    part = part + times(swap_ref[:, :depth], mown_ref[...]) + times(swap_ref[:, depth:], mother_ref[...])
    part = part.astype(BF)
    for k in range(n_x):
        out_ref[k] = part[k * rows : (k + 1) * rows]


def rows_product(which_core, low, diag, keep, mown, mother, n_x):
    n_ab, many, wide = low.shape
    width, depth = mown.shape
    step = 384
    block = pl.BlockSpec((step, depth), lambda n: (n, 0))
    return pl.pallas_call(
        rows_kernel,
        grid=(width // step,),
        out_shape=shape(n_x, many // n_x, width),
        in_specs=[
            SMEM,
            pl.BlockSpec((n_ab, many, wide), lambda n: (0, 0, 0)),
            pl.BlockSpec((many, 1), lambda n: (0, 0)),
            pl.BlockSpec((step, 2 * depth), lambda n: (n, 0)),
            block,
            block,
        ],
        out_specs=pl.BlockSpec((n_x, many // n_x, step), lambda n: (0, 0, n)),
        scratch_shapes=[pltpu.VMEM((many, 2 * depth), BF)] * 2,
        compiler_params=pltpu.CompilerParams(vmem_limit_bytes=LARGE),
        cost_estimate=pl.CostEstimate(flops=2 << 30, bytes_accessed=7 * MIB, transcendentals=0),
    )(which_core, low, diag, keep, mown, mother)


def sum_leading(ref):
    total = ref[0].astype(F32)
    for i in range(1, ref.shape[0]):
        total = total + ref[i].astype(F32)
    return total


def gather_sum_kernel(parts_hbm, out_ref, parts_ref, sems):
    pieces, rows, _ = out_ref.shape
    step = rows // 2
    chunks = [(j, slice(i * step, (i + 1) * step)) for j in range(pieces) for i in range(2)]
    copies = []
    for n, (j, here) in enumerate(chunks):
        copies.append(pltpu.make_async_copy(parts_hbm.at[:, j, here], parts_ref.at[:, j, here], sems.at[n]))
        copies[-1].start()
    for n, (j, here) in enumerate(chunks):
        copies[n].wait()
        total = parts_ref[0, j, here].astype(F32)
        for i in range(1, parts_ref.shape[0]):
            total = total + parts_ref[i, j, here].astype(F32)
        out_ref[j, here] = total.astype(BF)


def sum_sources(parts):
    return pl.pallas_call(
        gather_sum_kernel,
        out_shape=shape(*parts.shape[1:]),
        in_specs=[ANY],
        out_specs=VMEM,
        scratch_shapes=[pltpu.VMEM(parts.shape, BF), pltpu.SemaphoreType.DMA((2 * parts.shape[1],))],
        compiler_params=pltpu.CompilerParams(vmem_limit_bytes=WHOLE),
    )(parts)


def swap_rows(values, diagonal):
    rows = values.shape[0]
    up = pltpu.roll(values, rows - 1, 0)
    down = pltpu.roll(values, 1, 0)
    even = lax.broadcasted_iota(jnp.int32, values.shape, 0) % 2 == 0
    return jnp.where(diagonal != 0, values, jnp.where(even, up, down))


def open_columns_kernel(half_ref, pieces_ref, total_ref, same_ref, cross_ref):
    half = half_ref[0]
    total = sum_leading(pieces_ref)
    total_ref[...] = total
    low = total.astype(BF)
    middle = low.shape[0] // 2
    lane, out = iotas(BLK, BLK)
    for ref, which in ((same_ref, half), (cross_ref, 1 - half)):
        y = lane % SIDE
        place = y % 8 * 8 + lane // SIDE
        goes = y // 8 == which
        left = ones_where(goes & (out == place))
        right = ones_where(goes & (out == place + BLK // 2))
        packed = jnp.dot(low[:middle], left, preferred_element_type=F32)
        packed = packed + jnp.dot(low[middle:], right, preferred_element_type=F32)
        ref[...] = packed.astype(BF)


def close_columns_kernel(half_ref, total_ref, same_ref, cross_ref, driver_ref, den_ref, diag_ref, out_ref):
    half = half_ref[0]
    middle = same_ref.shape[0]
    lane, out = iotas(BLK, BLK)
    for part in range(2):
        rows = slice(part * middle, (part + 1) * middle)
        mirrored = 0.0
        for ref, which in ((same_ref, half), (cross_ref, 1 - half)):
            at = lane - part * (BLK // 2)
            inside = (at >= 0) & (at < BLK // 2)
            place = at // 8 * SIDE + which * 8 + at % 8
            spread = ones_where(inside & (out == place))
            mirrored = mirrored + jnp.dot(ref[...], spread, preferred_element_type=F32)
        mirrored = swap_rows(mirrored, diag_ref[rows, :])
        driver = driver_ref[rows, :].astype(F32)
        low = ((driver + (total_ref[rows, :] + mirrored)) / den_ref[rows, :]).astype(BF)
        for i in range(out_ref.shape[0]):
            out_ref[i, rows, :] = low


def open_rows_kernel(mine_ref, pieces_ref, total_ref, out_ref):
    mine = mine_ref[0]
    count, rows, half = out_ref.shape
    total = sum_leading(pieces_ref)
    total_ref[...] = total
    out_ref[mine] = jnp.zeros((rows, half), BF)
    for j in range(1, count):
        out_ref[lax.rem(mine + j, count)] = total[:, (j - 1) * half : j * half].astype(BF)


def close_rows_kernel(mine_ref, total_ref, tiles_ref, driver_ref, row_ref, col_ref, diag_ref, out_ref):
    mine = mine_ref[0]
    count, _, half = tiles_ref.shape
    area = 2 * half
    lane, out = iotas(area, area)
    turn = ones_where(lane == turned(out))
    for j in range(count):
        b = lax.rem(mine + j, count)
        if j == 0:
            symmetric = total_ref[:, (count - 1) * half :]
        else:
            own = total_ref[:, (j - 1) * half : j * half]
            theirs = swap_rows(tiles_ref[b].astype(F32), diag_ref[...])
            both = jnp.concatenate([theirs, own], axis=1)
            high = both.astype(BF)
            behind = jnp.dot(high, turn, preferred_element_type=F32)
            behind = behind + jnp.dot((both - high.astype(F32)).astype(BF), turn, preferred_element_type=F32)
            symmetric = jnp.where(mine < b, jnp.concatenate([own, theirs], axis=1), behind)
        here = pl.ds(pl.multiple_of(b * area, area), area)
        den = col_ref[:, here] - row_ref[...]
        out_ref[:, here] = (driver_ref[:, here] + symmetric) / den


def pick(table, index):
    hit = index[:, None] == jnp.arange(table.shape[0], dtype=jnp.int32)[None, :]
    return jnp.sum(jnp.where(hit, table[None, :], jnp.zeros((), table.dtype)), axis=1)


def body(amplitudes, driver, ladder, block_mask, pair_list, occ_energy, virt_energy):
    n_x, n_zh, n_core = lax.axis_size("x"), lax.axis_size("zh"), lax.axis_size("core")
    n_ab = lax.axis_size(AB)
    cells = n_x * n_zh
    core, ix, izh = lax.axis_index("core"), lax.axis_index("x"), lax.axis_index("zh")
    ab_index = lax.axis_index(AB)
    mine = ab_index.astype(jnp.int32).reshape(1)
    which_core = core.astype(jnp.int32).reshape(1)
    rows, cols = amplitudes.shape
    out_rows, in_cols = ladder.shape
    wide = cols // cells
    many = rows * cells
    area = SIDE * SIDE
    kept = (n_ab - 1) * (area // 2) + area
    swap_core = [(0, 1), (1, 0)]

    pack = pack_columns(amplitudes, driver, n_x, n_zh)
    pack = lax.all_to_all(pack.reshape(cells, rows, 2 * wide), GRID, 0, 0, tiled=True).reshape(many, 2 * wide)
    start = pack[:, :wide]
    drv = pack[:, wide:]

    other = lax.ppermute(ladder, "core", swap_core)
    other_mask = lax.ppermute(block_mask.T, "core", swap_core)
    _, other, other_mask, ladder = lax.optimization_barrier((pack, other, other_mask, ladder))
    own, other = mask_ladder(block_mask.T, other_mask, ladder, other)

    m = jnp.arange(many, dtype=jnp.int32)
    at = m // rows % n_zh * n_x + m // rows // n_zh
    local = pick(pair_list, (at * n_core + core) * rows + m % rows)
    row_energy = pick(occ_energy, local // NOCC) + pick(occ_energy, local % NOCC)
    diag = (local // NOCC == local % NOCC).astype(jnp.int32)
    pairs = ab_index * cols + jnp.arange(cols, dtype=jnp.int32)
    first = pairs // (SIDE * NV) * SIDE + pairs // SIDE % SIDE
    second = pairs // area % n_ab * SIDE + pairs % SIDE
    col_energy = pick(virt_energy, first) + pick(virt_energy, second)
    cell = izh * n_x + ix
    here = lax.dynamic_slice_in_dim(col_energy, cell * wide, wide)
    den = here[None, :] - row_energy[:, None]
    at = (ix * n_zh + izh) * rows
    my_rows = lax.dynamic_slice_in_dim(row_energy, at, rows)
    my_diag = lax.dynamic_slice_in_dim(diag, at, rows)
    half = (cell % 2).astype(jnp.int32).reshape(1)

    def place(a, q, c):
        return ((a * (n_zh * n_x)) + q) * n_core + c

    same, cross = [], []
    for a in range(n_ab):
        for q in range(cells):
            for c in range(n_core):
                b, h = q // 2, q % 2
                same.append((place(a, q, c), place(b, 2 * a + h, c)))
                cross.append((place(a, q, c), place(b, 2 * a + 1 - h, c)))

    low = lax.all_to_all(jnp.broadcast_to(start[None], (n_ab, many, wide)), AB, 0, 0, tiled=True)
    part = columns_product(which_core, low, own, other, n_x, n_zh)
    part, later = lax.optimization_barrier((part, own))
    part = lax.all_to_all(part, "x", 0, 0, tiled=True)

    turn, *send = call(
        send_kernel,
        (shape(area, in_cols),) + (shape(area // 2, in_cols),) * (n_ab - 1),
        [mine, later],
        1,
    )
    slots = [None] * n_ab

    def pass_on(j, block):
        slots[n_ab - j] = lax.ppermute(block, AB, [(k, (k + j) % n_ab) for k in range(n_ab)])

    early = [j for j in range(1, n_ab) if j % 2 or 2 * j == n_ab]
    for j in early:
        pass_on(j, send[j - 1])
    part, arrived, send = lax.optimization_barrier((part, [slots[n_ab - j] for j in early], send))
    for j, block in zip(early, arrived):
        slots[n_ab - j] = block

    part = lax.all_to_all(sum_sources(part), "zh", 0, 0, tiled=True)
    late = [j for j in range(1, n_ab) if j not in early]
    for j in late:
        pass_on(j, send[j - 1])
    part, arrived = lax.optimization_barrier((part, [slots[n_ab - j] for j in late]))
    for j, block in zip(late, arrived):
        slots[n_ab - j] = block
    mirror = call(join_kernel, shape(kept, in_cols), slots[1:] + [turn])
    mirror_other = lax.ppermute(mirror, "core", swap_core)

    total, to_same, to_cross = call(
        open_columns_kernel,
        (shape(many, wide, dtype=F32), shape(many // 2, wide), shape(many // 2, wide)),
        [half, part],
        1,
    )
    from_same = lax.ppermute(to_same, ALL, same)
    from_cross = lax.ppermute(to_cross, ALL, cross)
    low = call(
        close_columns_kernel,
        shape(n_ab, many, wide),
        [half, total, from_same, from_cross, drv, den, diag[:, None]],
        1,
    )

    low, later, later_other = lax.optimization_barrier((low, own, other))
    low = lax.all_to_all(low, AB, 0, 0, tiled=True)
    keep = call(keep_kernel, shape(kept, 2 * in_cols), [mine, later, later_other], 1, LARGE)
    part = rows_product(which_core, low, diag[:, None], keep, mirror, mirror_other, n_x)
    part = lax.all_to_all(part, "x", 0, 0, tiled=True)
    part = jnp.sum(part.astype(F32), axis=0).astype(BF).reshape(n_zh, rows, kept)
    part = lax.all_to_all(part, "zh", 0, 0, tiled=True)
    total, tiles = call(
        open_rows_kernel,
        (shape(rows, kept, dtype=F32), shape(n_ab, rows, area // 2)),
        [mine, part],
        1,
    )
    tiles = lax.all_to_all(tiles, AB, 0, 0, tiled=True)
    return call(
        close_rows_kernel,
        shape(rows, cols, dtype=F32),
        [mine, total, tiles, driver, my_rows[:, None], col_energy[None, :], my_diag[:, None]],
        1,
    )


def solution(mesh):
    fine = Mesh(mesh.devices.reshape(4, 2, 4, 4, 2), ALL)
    ab, cd = AB, ("zh", "x", "core")
    placed = (P(cd, ab), P(cd, ab), P(ab, cd), P(ab, cd), P(), P(), P())
    return jax.shard_map(body, mesh=fine, in_specs=placed, out_specs=P(cd, ab), check_vma=False)
```

```python
import jax
import jax.numpy as jnp
from jax import lax
from jax.experimental import pallas as pl
from jax.experimental.pallas import tpu as pltpu
from jax.sharding import Mesh, PartitionSpec as P

NV = 128
NOCC = 32
BLK = 128
SIDE = 16
BF = jnp.bfloat16
F32 = jnp.float32
AB = ("y", "zl")
GRID = ("x", "zh")
ALL = ("y", "zl", "zh", "x", "core")
VMEM = pl.BlockSpec(memory_space=pltpu.VMEM)
ANY = pl.BlockSpec(memory_space=pl.ANY)
SMEM = pl.BlockSpec(memory_space=pltpu.SMEM)
MIB = 1 << 20
SMALL = 12 * MIB
LARGE = 52 * MIB
WHOLE = 60 * MIB


def shape(*dims, dtype=BF):
    return jax.ShapeDtypeStruct(dims, dtype)


def call(kernel, out_shape, inputs, scalars=0, limit=SMALL):
    specs = [SMEM] * scalars + [VMEM] * (len(inputs) - scalars)
    outs = jax.tree.map(lambda _: VMEM, out_shape)
    return pl.pallas_call(
        kernel,
        out_shape=out_shape,
        in_specs=specs,
        out_specs=outs,
        compiler_params=pltpu.CompilerParams(vmem_limit_bytes=limit),
    )(*inputs)


def ones_where(condition):
    return condition.astype(F32).astype(BF)


def iotas(rows, cols):
    return (
        lax.broadcasted_iota(jnp.int32, (rows, cols), 0),
        lax.broadcasted_iota(jnp.int32, (rows, cols), 1),
    )


def turned(index):
    return index % SIDE * SIDE + index // SIDE


def pack_kernel(amplitudes_hbm, driver_hbm, out_ref, amplitudes_ref, driver_ref, sems):
    n_x, n_zh, _, width = out_ref.shape
    width = width // 2
    step = n_x * width
    copies = []
    for i in range(n_zh):
        here = slice(i * step, (i + 1) * step)
        copies.append(pltpu.make_async_copy(amplitudes_hbm.at[:, here], amplitudes_ref.at[:, here], sems.at[0, i]))
        copies.append(pltpu.make_async_copy(driver_hbm.at[:, here], driver_ref.at[:, here], sems.at[1, i]))
    for copy in copies:
        copy.start()
    for i in range(n_zh):
        copies[2 * i].wait()
        copies[2 * i + 1].wait()
        for x in range(n_x):
            here = slice((i * n_x + x) * width, (i * n_x + x + 1) * width)
            out_ref[x, i, :, :width] = amplitudes_ref[:, here].astype(BF)
            out_ref[x, i, :, width:] = driver_ref[:, here].astype(BF)


def pack_columns(amplitudes, driver, n_x, n_zh):
    rows, cols = amplitudes.shape
    return pl.pallas_call(
        pack_kernel,
        out_shape=shape(n_x, n_zh, rows, 2 * cols // (n_x * n_zh)),
        in_specs=[ANY, ANY],
        out_specs=VMEM,
        scratch_shapes=[pltpu.VMEM((rows, cols), F32)] * 2 + [pltpu.SemaphoreType.DMA((2, n_zh))],
        compiler_params=pltpu.CompilerParams(vmem_limit_bytes=WHOLE),
    )(amplitudes, driver)


def mask_kernel(mask_ref, other_mask_ref, ladder_ref, other_ref, out_ref, other_out_ref):
    step = pl.program_id(0) * (ladder_ref.shape[0] // BLK)
    for mask, source, out in ((mask_ref, ladder_ref, out_ref), (other_mask_ref, other_ref, other_out_ref)):
        for i in range(source.shape[0] // BLK):
            rows = slice(i * BLK, (i + 1) * BLK)
            for t in range(source.shape[1] // BLK):
                cols = slice(t * BLK, (t + 1) * BLK)
                block = source[rows, cols]
                out[rows, cols] = jnp.where(mask[t, step + i] != 0, block, jnp.zeros_like(block))


def mask_ladder(block_mask, other_mask, ladder, other):
    rows, cols = ladder.shape
    block = pl.BlockSpec((rows // 4, cols), lambda n: (n, 0))
    return pl.pallas_call(
        mask_kernel,
        grid=(4,),
        out_shape=(shape(rows, cols), shape(rows, cols)),
        in_specs=[SMEM, SMEM, block, block],
        out_specs=(block, block),
        compiler_params=pltpu.CompilerParams(vmem_limit_bytes=LARGE),
        cost_estimate=pl.CostEstimate(flops=1 << 20, bytes_accessed=8 * MIB, transcendentals=0),
    )(block_mask, other_mask, ladder, other)


def send_kernel(mine_ref, masked_ref, turn_ref, *send_refs):
    mine = mine_ref[0]
    area = SIDE * SIDE
    half = area // 2
    count = masked_ref.shape[0] // area
    row, col = iotas(half, area)
    full_row, full_col = iotas(area, area)
    for j in range(count):
        b = lax.rem(mine + j, count)
        tile = masked_ref[pl.ds(pl.multiple_of(b * area, area), area), :]
        if j == 0:
            turn = ones_where(full_col == turned(full_row))
            turn_ref[...] = jnp.dot(turn, tile, preferred_element_type=F32).astype(BF)
        else:
            sent = ones_where(col == jnp.where(mine < b, half + row, turned(row)))
            send_refs[j - 1][...] = jnp.dot(sent, tile, preferred_element_type=F32).astype(BF)


def join_kernel(*refs):
    out_ref = refs[-1]
    at = 0
    for ref in refs[:-1]:
        out_ref[at : at + ref.shape[0], :] = ref[...]
        at += ref.shape[0]


def keep_kernel(mine_ref, own_ref, other_ref, keep_ref):
    mine = mine_ref[0]
    area = SIDE * SIDE
    half = area // 2
    count = own_ref.shape[0] // area
    depth = own_ref.shape[1]
    row, col = iotas(half, area)
    for j in range(count):
        b = lax.rem(mine + j, count)
        kept = ones_where(col == jnp.where(mine < b, row, turned(half + row)))
        for i, ref in enumerate((own_ref, other_ref)):
            cols = slice(i * depth, (i + 1) * depth)
            tile = ref[pl.ds(pl.multiple_of(b * area, area), area), :]
            if j == 0:
                keep_ref[(count - 1) * half :, cols] = tile
            else:
                keep_ref[(j - 1) * half : j * half, cols] = jnp.dot(
                    kept, tile, preferred_element_type=F32
                ).astype(BF)


def times(left, right):
    return lax.dot_general(left, right, (((1,), (1,)), ((), ())), preferred_element_type=F32)


def store_halves(core_ref, low_ref, out_ref):
    first = core_ref[0] == 0
    half = BLK // 2
    count = low_ref.shape[0]
    for s in range(0, count, 2):
        a, b = low_ref[s], low_ref[s + 1]
        zero = jnp.concatenate([a[:, :half], b[:, :half]], axis=1)
        one = jnp.concatenate([a[:, half:], b[:, half:]], axis=1)
        out_ref[:, s // 2 * BLK : (s // 2 + 1) * BLK] = jnp.where(first, zero, one)
        at = (count + s) // 2 * BLK
        out_ref[:, at : at + BLK] = jnp.where(first, one, zero)


def columns_kernel(core_ref, low_ref, own_ref, other_ref, out_ref, held_ref):
    depth = own_ref.shape[1]

    @pl.when(pl.program_id(0) == 0)
    def _():
        store_halves(core_ref, low_ref, held_ref)

    count = out_ref.shape[0] * out_ref.shape[1]
    part = times(held_ref[:, :depth], own_ref[...]) + times(held_ref[:, depth:], other_ref[...])
    part = part.astype(BF)
    for j in range(count):
        out_ref[j % out_ref.shape[0], j // out_ref.shape[0]] = part[:, j * BLK : (j + 1) * BLK]


def columns_product(which_core, low, own, other, n_x, n_zh):
    n_ab, many, wide = low.shape
    out_rows, depth = own.shape
    steps = 2
    block = pl.BlockSpec((out_rows // steps, depth), lambda n: (n, 0))
    return pl.pallas_call(
        columns_kernel,
        grid=(steps,),
        out_shape=shape(n_x, n_zh, many, wide),
        in_specs=[SMEM, pl.BlockSpec((n_ab, many, wide), lambda n: (0, 0, 0)), block, block],
        out_specs=pl.BlockSpec((n_x, n_zh // steps, many, wide), lambda n: (0, n, 0, 0)),
        scratch_shapes=[pltpu.VMEM((many, 2 * depth), BF)],
        compiler_params=pltpu.CompilerParams(vmem_limit_bytes=LARGE),
        cost_estimate=pl.CostEstimate(flops=2 << 30, bytes_accessed=7 * MIB, transcendentals=0),
    )(which_core, low, own, other)


def rows_kernel(core_ref, low_ref, diag_ref, keep_ref, mown_ref, mother_ref, out_ref, held_ref, swap_ref):
    n_x, rows, _ = out_ref.shape
    depth = mown_ref.shape[1]

    @pl.when(pl.program_id(0) == 0)
    def _():
        store_halves(core_ref, low_ref, held_ref)
        row, col = iotas(BLK, BLK)
        other = row + 1 - 2 * (row % 2)
        for i in range(held_ref.shape[0] // BLK):
            here = slice(i * BLK, (i + 1) * BLK)
            swap = ones_where(col == jnp.where(diag_ref[here, :] != 0, row, other))
            swap_ref[here, :] = jnp.dot(swap, held_ref[here, :], preferred_element_type=F32).astype(BF)

    part = times(held_ref[...], keep_ref[...])
    part = part + times(swap_ref[:, :depth], mown_ref[...]) + times(swap_ref[:, depth:], mother_ref[...])
    part = part.astype(BF)
    for k in range(n_x):
        out_ref[k] = part[k * rows : (k + 1) * rows]


def rows_product(which_core, low, diag, keep, mown, mother, n_x):
    n_ab, many, wide = low.shape
    width, depth = mown.shape
    step = 384
    block = pl.BlockSpec((step, depth), lambda n: (n, 0))
    return pl.pallas_call(
        rows_kernel,
        grid=(width // step,),
        out_shape=shape(n_x, many // n_x, width),
        in_specs=[
            SMEM,
            pl.BlockSpec((n_ab, many, wide), lambda n: (0, 0, 0)),
            pl.BlockSpec((many, 1), lambda n: (0, 0)),
            pl.BlockSpec((step, 2 * depth), lambda n: (n, 0)),
            block,
            block,
        ],
        out_specs=pl.BlockSpec((n_x, many // n_x, step), lambda n: (0, 0, n)),
        scratch_shapes=[pltpu.VMEM((many, 2 * depth), BF)] * 2,
        compiler_params=pltpu.CompilerParams(vmem_limit_bytes=LARGE),
        cost_estimate=pl.CostEstimate(flops=2 << 30, bytes_accessed=7 * MIB, transcendentals=0),
    )(which_core, low, diag, keep, mown, mother)


def sum_leading(ref):
    total = ref[0].astype(F32)
    for i in range(1, ref.shape[0]):
        total = total + ref[i].astype(F32)
    return total


def gather_sum_kernel(parts_hbm, out_ref, parts_ref, sems):
    pieces, rows, _ = out_ref.shape
    step = rows // 2
    chunks = [(j, slice(i * step, (i + 1) * step)) for j in range(pieces) for i in range(2)]
    copies = []
    for n, (j, here) in enumerate(chunks):
        copies.append(pltpu.make_async_copy(parts_hbm.at[:, j, here], parts_ref.at[:, j, here], sems.at[n]))
        copies[-1].start()
    for n, (j, here) in enumerate(chunks):
        copies[n].wait()
        total = parts_ref[0, j, here].astype(F32)
        for i in range(1, parts_ref.shape[0]):
            total = total + parts_ref[i, j, here].astype(F32)
        out_ref[j, here] = total.astype(BF)


def sum_sources(parts):
    return pl.pallas_call(
        gather_sum_kernel,
        out_shape=shape(*parts.shape[1:]),
        in_specs=[ANY],
        out_specs=VMEM,
        scratch_shapes=[pltpu.VMEM(parts.shape, BF), pltpu.SemaphoreType.DMA((2 * parts.shape[1],))],
        compiler_params=pltpu.CompilerParams(vmem_limit_bytes=WHOLE),
    )(parts)


def swap_rows(values, diagonal):
    rows = values.shape[0]
    up = pltpu.roll(values, rows - 1, 0)
    down = pltpu.roll(values, 1, 0)
    even = lax.broadcasted_iota(jnp.int32, values.shape, 0) % 2 == 0
    return jnp.where(diagonal != 0, values, jnp.where(even, up, down))


def open_columns_kernel(half_ref, pieces_ref, total_ref, same_ref, cross_ref):
    half = half_ref[0]
    total = sum_leading(pieces_ref)
    total_ref[...] = total
    low = total.astype(BF)
    middle = low.shape[0] // 2
    lane, out = iotas(BLK, BLK)
    for ref, which in ((same_ref, half), (cross_ref, 1 - half)):
        y = lane % SIDE
        place = y % 8 * 8 + lane // SIDE
        goes = y // 8 == which
        left = ones_where(goes & (out == place))
        right = ones_where(goes & (out == place + BLK // 2))
        packed = jnp.dot(low[:middle], left, preferred_element_type=F32)
        packed = packed + jnp.dot(low[middle:], right, preferred_element_type=F32)
        ref[...] = packed.astype(BF)


def close_columns_kernel(half_ref, total_ref, same_ref, cross_ref, driver_ref, den_ref, diag_ref, out_ref):
    half = half_ref[0]
    middle = same_ref.shape[0]
    lane, out = iotas(BLK, BLK)
    for part in range(2):
        rows = slice(part * middle, (part + 1) * middle)
        mirrored = 0.0
        for ref, which in ((same_ref, half), (cross_ref, 1 - half)):
            at = lane - part * (BLK // 2)
            inside = (at >= 0) & (at < BLK // 2)
            place = at // 8 * SIDE + which * 8 + at % 8
            spread = ones_where(inside & (out == place))
            mirrored = mirrored + jnp.dot(ref[...], spread, preferred_element_type=F32)
        mirrored = swap_rows(mirrored, diag_ref[rows, :])
        driver = driver_ref[rows, :].astype(F32)
        low = ((driver + (total_ref[rows, :] + mirrored)) / den_ref[rows, :]).astype(BF)
        for i in range(out_ref.shape[0]):
            out_ref[i, rows, :] = low


def open_rows_kernel(mine_ref, pieces_ref, total_ref, out_ref):
    mine = mine_ref[0]
    count, rows, half = out_ref.shape
    total = sum_leading(pieces_ref)
    total_ref[...] = total
    out_ref[mine] = jnp.zeros((rows, half), BF)
    for j in range(1, count):
        out_ref[lax.rem(mine + j, count)] = total[:, (j - 1) * half : j * half].astype(BF)


def close_rows_kernel(mine_ref, total_ref, tiles_ref, driver_ref, row_ref, col_ref, diag_ref, out_ref):
    mine = mine_ref[0]
    count, _, half = tiles_ref.shape
    area = 2 * half
    lane, out = iotas(area, area)
    turn = ones_where(lane == turned(out))
    for j in range(count):
        b = lax.rem(mine + j, count)
        if j == 0:
            symmetric = total_ref[:, (count - 1) * half :]
        else:
            own = total_ref[:, (j - 1) * half : j * half]
            theirs = swap_rows(tiles_ref[b].astype(F32), diag_ref[...])
            both = jnp.concatenate([theirs, own], axis=1)
            high = both.astype(BF)
            behind = jnp.dot(high, turn, preferred_element_type=F32)
            behind = behind + jnp.dot((both - high.astype(F32)).astype(BF), turn, preferred_element_type=F32)
            symmetric = jnp.where(mine < b, jnp.concatenate([own, theirs], axis=1), behind)
        here = pl.ds(pl.multiple_of(b * area, area), area)
        den = col_ref[:, here] - row_ref[...]
        out_ref[:, here] = (driver_ref[:, here] + symmetric) / den


def pick(table, index):
    hit = index[:, None] == jnp.arange(table.shape[0], dtype=jnp.int32)[None, :]
    return jnp.sum(jnp.where(hit, table[None, :], jnp.zeros((), table.dtype)), axis=1)


def body(amplitudes, driver, ladder, block_mask, pair_list, occ_energy, virt_energy):
    n_x, n_zh, n_core = lax.axis_size("x"), lax.axis_size("zh"), lax.axis_size("core")
    n_ab = lax.axis_size(AB)
    cells = n_x * n_zh
    core, ix, izh = lax.axis_index("core"), lax.axis_index("x"), lax.axis_index("zh")
    ab_index = lax.axis_index(AB)
    mine = ab_index.astype(jnp.int32).reshape(1)
    which_core = core.astype(jnp.int32).reshape(1)
    rows, cols = amplitudes.shape
    out_rows, in_cols = ladder.shape
    wide = cols // cells
    many = rows * cells
    area = SIDE * SIDE
    kept = (n_ab - 1) * (area // 2) + area
    swap_core = [(0, 1), (1, 0)]

    pack = pack_columns(amplitudes, driver, n_x, n_zh)
    pack = lax.all_to_all(pack.reshape(cells, rows, 2 * wide), GRID, 0, 0, tiled=True).reshape(many, 2 * wide)
    start = pack[:, :wide]
    drv = pack[:, wide:]

    other = lax.ppermute(ladder, "core", swap_core)
    other_mask = lax.ppermute(block_mask.T, "core", swap_core)
    _, other, other_mask, ladder = lax.optimization_barrier((pack, other, other_mask, ladder))
    own, other = mask_ladder(block_mask.T, other_mask, ladder, other)

    m = jnp.arange(many, dtype=jnp.int32)
    at = m // rows % n_zh * n_x + m // rows // n_zh
    local = pick(pair_list, (at * n_core + core) * rows + m % rows)
    row_energy = pick(occ_energy, local // NOCC) + pick(occ_energy, local % NOCC)
    diag = (local // NOCC == local % NOCC).astype(jnp.int32)
    pairs = ab_index * cols + jnp.arange(cols, dtype=jnp.int32)
    first = pairs // (SIDE * NV) * SIDE + pairs // SIDE % SIDE
    second = pairs // area % n_ab * SIDE + pairs % SIDE
    col_energy = pick(virt_energy, first) + pick(virt_energy, second)
    cell = izh * n_x + ix
    here = lax.dynamic_slice_in_dim(col_energy, cell * wide, wide)
    den = here[None, :] - row_energy[:, None]
    at = (ix * n_zh + izh) * rows
    my_rows = lax.dynamic_slice_in_dim(row_energy, at, rows)
    my_diag = lax.dynamic_slice_in_dim(diag, at, rows)
    half = (cell % 2).astype(jnp.int32).reshape(1)

    def place(a, q, c):
        return ((a * (n_zh * n_x)) + q) * n_core + c

    same, cross = [], []
    for a in range(n_ab):
        for q in range(cells):
            for c in range(n_core):
                b, h = q // 2, q % 2
                same.append((place(a, q, c), place(b, 2 * a + h, c)))
                cross.append((place(a, q, c), place(b, 2 * a + 1 - h, c)))

    low = lax.all_to_all(jnp.broadcast_to(start[None], (n_ab, many, wide)), AB, 0, 0, tiled=True)
    part = columns_product(which_core, low, own, other, n_x, n_zh)
    part, later = lax.optimization_barrier((part, own))
    part = lax.all_to_all(part, "x", 0, 0, tiled=True)

    turn, *send = call(
        send_kernel,
        (shape(area, in_cols),) + (shape(area // 2, in_cols),) * (n_ab - 1),
        [mine, later],
        1,
    )
    slots = [None] * n_ab

    def pass_on(j, block):
        slots[n_ab - j] = lax.ppermute(block, AB, [(k, (k + j) % n_ab) for k in range(n_ab)])

    early = [j for j in range(1, n_ab) if j % 2 or 2 * j == n_ab]
    for j in early:
        pass_on(j, send[j - 1])
    part = sum_sources(part)
    part, arrived, send = lax.optimization_barrier((part, [slots[n_ab - j] for j in early], send))
    for j, block in zip(early, arrived):
        slots[n_ab - j] = block

    part = lax.all_to_all(part, "zh", 0, 0, tiled=True)
    late = [j for j in range(1, n_ab) if j not in early]
    for j in late:
        pass_on(j, send[j - 1])
    part, arrived = lax.optimization_barrier((part, [slots[n_ab - j] for j in late]))
    for j, block in zip(late, arrived):
        slots[n_ab - j] = block
    mirror = call(join_kernel, shape(kept, in_cols), slots[1:] + [turn])
    mirror_other = lax.ppermute(mirror, "core", swap_core)

    total, to_same, to_cross = call(
        open_columns_kernel,
        (shape(many, wide, dtype=F32), shape(many // 2, wide), shape(many // 2, wide)),
        [half, part],
        1,
    )
    from_same = lax.ppermute(to_same, ALL, same)
    from_cross = lax.ppermute(to_cross, ALL, cross)
    low = call(
        close_columns_kernel,
        shape(n_ab, many, wide),
        [half, total, from_same, from_cross, drv, den, diag[:, None]],
        1,
    )

    low, later, later_other = lax.optimization_barrier((low, own, other))
    low = lax.all_to_all(low, AB, 0, 0, tiled=True)
    keep = call(keep_kernel, shape(kept, 2 * in_cols), [mine, later, later_other], 1, LARGE)
    part = rows_product(which_core, low, diag[:, None], keep, mirror, mirror_other, n_x)
    part = lax.all_to_all(part, "x", 0, 0, tiled=True)
    part = jnp.sum(part.astype(F32), axis=0).astype(BF).reshape(n_zh, rows, kept)
    part = lax.all_to_all(part, "zh", 0, 0, tiled=True)
    total, tiles = call(
        open_rows_kernel,
        (shape(rows, kept, dtype=F32), shape(n_ab, rows, area // 2)),
        [mine, part],
        1,
    )
    tiles = lax.all_to_all(tiles, AB, 0, 0, tiled=True)
    return call(
        close_rows_kernel,
        shape(rows, cols, dtype=F32),
        [mine, total, tiles, driver, my_rows[:, None], col_energy[None, :], my_diag[:, None]],
        1,
    )


def solution(mesh):
    fine = Mesh(mesh.devices.reshape(4, 2, 4, 4, 2), ALL)
    ab, cd = AB, ("zh", "x", "core")
    placed = (P(cd, ab), P(cd, ab), P(ab, cd), P(ab, cd), P(), P(), P())
    return jax.shard_map(body, mesh=fine, in_specs=placed, out_specs=P(cd, ab), check_vma=False)
```
